256 devices in a mesh: seq: 256 (over y, x, z, core).
Axes of the slice: x: 4, y: 4, z: 8, core: 2. Of those that a mesh axis runs over, the one named last changes fastest.
Arguments:
- signal: float32 [262144, 256], P('seq'), may hold values from -6 to 6
- conv_weight: bfloat16 [6, 768, 512], replicated, may hold values from -0.21875 to 0.21875
- conv_bias: float32 [6, 512], replicated, may hold values from -3 to 3
- res_weight: bfloat16 [6, 256, 256], replicated, may hold values from -0.375 to 0.375
- skip_weight: bfloat16 [6, 256, 256], replicated, may hold values from -0.375 to 0.375
Outputs:
- features: float32 [262144, 256], P('seq')
- skip_sum: float32 [262144, 256], P('seq')
The draws below stay inside these ranges and needn't reach their ends.
All inputs are finite; a program needn't handle non-finite values.
Results may differ from the reference program's by a relative error of at most 0.0051.
Values may be sent and summed in bfloat16 or wider, within the bound.
A program may use at most 64 MiB of HBM per device.

```python
import jax
import jax.numpy as jnp

C = 256
H = 512
LAYERS = 6
FIRST_DILATION = 512
SEQUENCE_LENGTH = 262144


def block_scale(own_key, extent, shards, low, top_value):
    factor_of, own = 1.0, jax.random.fold_in(own_key, 6)
    for dim, parts in shards:
        draws = jnp.exp(jax.random.uniform(jax.random.fold_in(own, dim), (parts,), jnp.float32, low / len(shards), top_value / len(shards)))
        factor_of = factor_of * jnp.repeat(draws, extent[dim] // parts).reshape([-1 if axis == dim else 1 for axis in range(len(extent))])
    return factor_of


def bell_draw(own_key, dims, deviation, most, cuts=(), held_as=jnp.bfloat16):
    result = jax.random.normal(own_key, dims, jnp.float32) * deviation
    if len(cuts) > 0:
        result = block_scale(own_key, dims, cuts, -0.22, 0.18) * result
    return jnp.clip(result, min=-most, max=most).astype(held_as)


def setup_inputs(seed: int = 0) -> dict:
    key_list = jax.random.split(jax.random.key(seed), 6)
    signal = bell_draw(key_list[0], (SEQUENCE_LENGTH, C), 1.0, 6.0, ((0, 256),), jnp.float32)
    conv_weight = bell_draw(key_list[1], (LAYERS, 3 * C, H), (3 * C) ** -0.5, 0.21875)
    conv_bias = bell_draw(key_list[2], (LAYERS, H), 0.5, 3.0, (), jnp.float32)
    res_weight = bell_draw(key_list[3], (LAYERS, C, C), C ** -0.5, 0.375)
    skip_weight = bell_draw(key_list[4], (LAYERS, C, C), C ** -0.5, 0.375)
    return {"signal": signal, "conv_weight": conv_weight, "conv_bias": conv_bias, "res_weight": res_weight, "skip_weight": skip_weight}


def reference(signal, conv_weight, conv_bias, res_weight, skip_weight):
    current = signal
    skip_sum = jnp.zeros_like(signal)
    for index_of_layer in range(LAYERS):
        shifted_rows = FIRST_DILATION * 2 ** index_of_layer
        rounded = current.astype(jnp.bfloat16)
        padding = jnp.zeros((shifted_rows, C), jnp.bfloat16)
        before_rows = jnp.concatenate([padding, rounded[:-shifted_rows]], 0)
        following_rows = jnp.concatenate([rounded[shifted_rows:], padding], 0)
        weights = conv_weight[index_of_layer]
        pre_gate = jnp.dot(before_rows, weights[:C], preferred_element_type=jnp.float32)
        pre_gate = pre_gate + jnp.dot(rounded, weights[C:2 * C], preferred_element_type=jnp.float32)
        pre_gate = pre_gate + jnp.dot(following_rows, weights[2 * C:], preferred_element_type=jnp.float32)
        pre_gate = pre_gate + conv_bias[index_of_layer]
        gated = (jnp.tanh(pre_gate[:, :C]) * jax.nn.sigmoid(pre_gate[:, C:])).astype(jnp.bfloat16)
        current = current + jnp.dot(gated, res_weight[index_of_layer], preferred_element_type=jnp.float32)
        skip_sum = skip_sum + jnp.dot(gated, skip_weight[index_of_layer], preferred_element_type=jnp.float32)
    return current, skip_sum
```

```python
import jax
import jax.numpy as jnp
from jax import lax
from jax.sharding import PartitionSpec as P

LAYERS = 6
FIRST_DILATION = 512


def shifted(value, rows):
    padding = jnp.zeros((abs(rows),) + value.shape[1:], value.dtype)
    if rows > 0:
        return jnp.concatenate([padding, value[:-rows]], 0)
    return jnp.concatenate([value[-rows:], padding], 0)


def body(devices, signal, conv_weight, conv_bias, res_weight, skip_weight):
    row_count, channels = signal.shape
    halves = row_count // FIRST_DILATION
    own = FIRST_DILATION // devices
    sent = signal.astype(jnp.bfloat16).reshape(halves, devices, own, channels).transpose(1, 0, 2, 3)
    taken = lax.all_to_all(sent.reshape(devices, halves * own, channels), "seq", 0, 0, tiled=True)
    start = taken.reshape(row_count, channels).astype(jnp.float32)
    delta = jnp.zeros_like(start)
    skip_sum = jnp.zeros_like(start)
    for layer in range(LAYERS):
        rounded = (start + delta).astype(jnp.bfloat16)
        step = own * 2**layer
        joined = jnp.concatenate([shifted(rounded, step), rounded, shifted(rounded, -step)], 1)
        pre_gate = jnp.dot(joined, conv_weight[layer], preferred_element_type=jnp.float32) + conv_bias[layer]
        gated = (jnp.tanh(pre_gate[:, :channels]) * jax.nn.sigmoid(pre_gate[:, channels:])).astype(jnp.bfloat16)
        delta = delta + jnp.dot(gated, res_weight[layer], preferred_element_type=jnp.float32)
        skip_sum = skip_sum + jnp.dot(gated, skip_weight[layer], preferred_element_type=jnp.float32)
    both = jnp.concatenate([delta, skip_sum], 1).astype(jnp.bfloat16)
    back = lax.all_to_all(both.reshape(devices, halves * own, 2 * channels), "seq", 0, 0, tiled=True)
    back = back.reshape(devices, halves, own, 2 * channels).transpose(1, 0, 2, 3).reshape(row_count, 2 * channels)
    back = back.astype(jnp.float32)
    return signal + back[:, :channels], back[:, channels:]


def solution(mesh):
    devices = mesh.shape["seq"]
    in_specs = (P("seq", None), P(), P(), P(), P())
    out_specs = (P("seq", None), P("seq", None))

    def run(*args):
        return body(devices, *args)

    return jax.shard_map(run, mesh=mesh, in_specs=in_specs, out_specs=out_specs, check_vma=False)
```

```python
import jax
import jax.numpy as jnp
from jax import lax
from jax.experimental import pallas as pl
from jax.experimental.pallas import tpu as pltpu
from jax.sharding import PartitionSpec as P

LAYERS = 6
HALVES = 2
RESIDUES = 512
GROUP = 16
CHUNKS = 2
LENGTH = 512
C = 256
PAD = 32
TILE = 256
MESH = pl.DeviceIdType.MESH
BF16 = jnp.bfloat16
F32 = jnp.float32

ALONG_Z = [(dz, dc) for dz in (1, 7, 2, 6, 3, 5, 4, 0) for dc in (0, 1) if (dz, dc) != (0, 0)]
ACROSS = [(dy, dx) for dy in (0, 1, 3, 2) for dx in (1, 3, 2, 0) if (dy, dx) != (0, 0)]


def kernel(
    signal_hbm,
    conv_hbm,
    bias_ref,
    res_hbm,
    skip_hbm,
    delta_out,
    skip_out,
    signal,
    conv,
    proj,
    sent,
    perm,
    perm_t,
    r1,
    t1,
    r2,
    t2,
    r3,
    t3,
    cur,
    skip,
    x3,
    load_sem,
    weight_sem,
    send_sem,
    in_z_sem,
    in_xy_sem,
    out_xy_sem,
    out_z_sem,
    own_sem,
):
    me = lax.axis_index("seq")
    j, g = lax.rem(me, GROUP), me // GROUP
    z, core = j // 2, lax.rem(j, 2)
    y, x = g // 4, lax.rem(g, 4)
    z_peers = [lax.rem(z + dz, 8) * 2 + lax.rem(core + dc, 2) for dz, dc in ALONG_Z]
    xy_peers = [lax.rem(y + dy, 4) * 4 + lax.rem(x + dx, 4) for dy, dx in ACROSS]

    barrier = pltpu.get_barrier_semaphore()
    for peer in z_peers:
        pl.semaphore_signal(barrier, inc=1, device_id=(g * GROUP + peer,), device_id_type=MESH)
    for peer in xy_peers:
        pl.semaphore_signal(barrier, inc=1, device_id=(peer * GROUP + j,), device_id_type=MESH)

    load = pltpu.make_async_copy(signal_hbm, signal, load_sem)
    load.start()
    weights = [
        pltpu.make_async_copy(conv_hbm, conv, weight_sem.at[0]),
        pltpu.make_async_copy(res_hbm, proj.at[:, :, pl.ds(0, C)], weight_sem.at[1]),
        pltpu.make_async_copy(skip_hbm, proj.at[:, :, pl.ds(C, C)], weight_sem.at[2]),
    ]
    for copy in weights:
        copy.start()
    row = lax.broadcasted_iota(jnp.int32, (LENGTH, LENGTH), 0)
    col = lax.broadcasted_iota(jnp.int32, (LENGTH, LENGTH), 1)
    perm[...] = jnp.where(col == (row & 31) * 16 + (row >> 5), 1.0, 0.0).astype(BF16)
    perm_t[...] = jnp.where(row == (col & 31) * 16 + (col >> 5), 1.0, 0.0).astype(BF16)
    cur[pl.ds(0, PAD), :] = jnp.zeros((PAD, C), F32)
    cur[pl.ds(PAD + LENGTH, PAD), :] = jnp.zeros((PAD, C), F32)
    load.wait()
    sent[...] = signal[...].astype(BF16)
    pl.semaphore_wait(barrier, 2 * (GROUP - 1))

    def rows_of(s, peer):
        return pl.ds(pl.multiple_of(s * 256 + peer * 16, 16), 16)

    def send(src, dst, stage, recv, device):
        pltpu.make_async_remote_copy(
            src_ref=src,
            dst_ref=dst,
            send_sem=send_sem.at[stage],
            recv_sem=recv,
            device_id=(device,),
            device_id_type=MESH,
        ).start()

    def arrived(buffer, sem):
        part = buffer.at[pl.ds(0, GROUP - 1)]
        pltpu.make_async_copy(part, part, sem).wait()

    for s in range(CHUNKS):
        for peer in z_peers:
            send(sent.at[:, rows_of(s, peer), :], r1.at[s, j], s, in_z_sem.at[s], g * GROUP + peer)
        r1[s, j] = sent[:, rows_of(s, j), :]

    def spread(s):
        arrived(r1.at[s], in_z_sem.at[s])
        rows = jnp.dot(perm[...], r1[s].reshape(LENGTH, C), preferred_element_type=F32)
        t1[s] = rows.astype(BF16).reshape(GROUP, 32, C)
        for peer in xy_peers:
            send(t1.at[s, peer], r2.at[s, g], 2 + s, in_xy_sem.at[s], peer * GROUP + j)
        r2[s, g] = t1[s, g]

    def layers(s):
        arrived(r2.at[s], in_xy_sem.at[s])
        cur[pl.ds(PAD, LENGTH), :] = r2[s].reshape(LENGTH, C).astype(F32)
        for layer in range(LAYERS):
            d = 2**layer
            for tap in range(3):
                x3[:, pl.ds(tap * C, C)] = cur[pl.ds(PAD + (tap - 1) * d, LENGTH), :].astype(BF16)
            for tile in range(LENGTH // TILE):
                at = pl.ds(tile * TILE, TILE)
                pre = jnp.dot(x3[at, :], conv[layer], preferred_element_type=F32)
                pre = pre + bias_ref[pl.ds(layer, 1), :]
                gated = (jnp.tanh(pre[:, :C]) * (0.5 + 0.5 * jnp.tanh(0.5 * pre[:, C:]))).astype(BF16)
                both = jnp.dot(gated, proj[layer], preferred_element_type=F32)
                at_cur = pl.ds(PAD + tile * TILE, TILE)
                if layer < LAYERS - 1:
                    cur[at_cur, :] = cur[at_cur, :] + both[:, :C]
                    skip[at, :] = both[:, C:] if layer == 0 else skip[at, :] + both[:, C:]
                else:
                    slots = pl.ds(tile * TILE // 32, TILE // 32)
                    start = r2[s, slots].reshape(TILE, C).astype(F32)
                    delta = (cur[at_cur, :] - start) + both[:, :C]
                    t2[s, 0, slots] = delta.astype(BF16).reshape(TILE // 32, 32, C)
                    total = skip[at, :] + both[:, C:]
                    t2[s, 1, slots] = total.astype(BF16).reshape(TILE // 32, 32, C)
        for part in range(2):
            for peer in xy_peers:
                send(
                    t2.at[s, part, peer],
                    r3.at[s, part, g],
                    4 + 2 * s + part,
                    out_xy_sem.at[2 * s + part],
                    peer * GROUP + j,
                )
            r3[s, part, g] = t2[s, part, g]

    own = []
    outs = (delta_out, skip_out)

    def give_back(s, part):
        arrived(r3.at[s, part], out_xy_sem.at[2 * s + part])
        rows = jnp.dot(perm_t[...], r3[s, part].reshape(LENGTH, C), preferred_element_type=F32)
        t3[s, part] = rows.astype(BF16).reshape(GROUP, HALVES, 16, C)
        for peer in z_peers:
            send(
                t3.at[s, part, peer],
                outs[part].at[:, rows_of(s, j), :],
                8 + 2 * s + part,
                out_z_sem.at[2 * s + part],
                g * GROUP + peer,
            )
        copy = pltpu.make_async_copy(
            t3.at[s, part, j], outs[part].at[:, rows_of(s, j), :], own_sem.at[2 * s + part]
        )
        copy.start()
        own.append(copy)

    spread(0)
    for copy in weights:
        copy.wait()
    layers(0)
    spread(1)
    give_back(0, 0)
    give_back(0, 1)
    layers(1)
    give_back(1, 0)
    give_back(1, 1)

    for s in range(CHUNKS):
        for part in range(2):
            arrived(t3.at[s, part], out_z_sem.at[2 * s + part])
    for copy in own:
        copy.wait()
    for stage in range(12):
        arrived(t1.at[0], send_sem.at[stage])


def body(signal, conv_weight, conv_bias, res_weight, skip_weight):
    any_space = pl.BlockSpec(memory_space=pl.ANY)
    slab = (CHUNKS, GROUP, 32, C)
    delta, skip_sum = pl.pallas_call(
        kernel,
        out_shape=[jax.ShapeDtypeStruct((HALVES, RESIDUES, C), BF16)] * 2,
        in_specs=[any_space, any_space, pl.BlockSpec(memory_space=pltpu.VMEM), any_space, any_space],
        out_specs=[any_space, any_space],
        scratch_shapes=[
            pltpu.VMEM((HALVES, RESIDUES, C), F32),
            pltpu.VMEM((LAYERS, 3 * C, 2 * C), BF16),
            pltpu.VMEM((LAYERS, C, 2 * C), BF16),
            pltpu.VMEM((HALVES, RESIDUES, C), BF16),
            pltpu.VMEM((LENGTH, LENGTH), BF16),
            pltpu.VMEM((LENGTH, LENGTH), BF16),
            pltpu.VMEM((CHUNKS, GROUP, HALVES, 16, C), BF16),
            pltpu.VMEM(slab, BF16),
            pltpu.VMEM(slab, BF16),
            pltpu.VMEM((CHUNKS, 2, GROUP, 32, C), BF16),
            pltpu.VMEM((CHUNKS, 2, GROUP, 32, C), BF16),
            pltpu.VMEM((CHUNKS, 2, GROUP, HALVES, 16, C), BF16),
            pltpu.VMEM((LENGTH + 2 * PAD, C), F32),
            pltpu.VMEM((LENGTH, C), F32),
            pltpu.VMEM((LENGTH, 3 * C), BF16),
            pltpu.SemaphoreType.DMA,
            pltpu.SemaphoreType.DMA((3,)),
            pltpu.SemaphoreType.DMA((12,)),
            pltpu.SemaphoreType.DMA((2,)),
            pltpu.SemaphoreType.DMA((2,)),
            pltpu.SemaphoreType.DMA((4,)),
            pltpu.SemaphoreType.DMA((4,)),
            pltpu.SemaphoreType.DMA((4,)),
        ],
        compiler_params=pltpu.CompilerParams(
            collective_id=0, has_side_effects=True, vmem_limit_bytes=60 * 2**20
        ),
    )(
        signal.reshape(HALVES, RESIDUES, C),
        conv_weight,
        conv_bias,
        res_weight,
        skip_weight,
    )
    shape = signal.shape
    return signal + delta.reshape(shape).astype(F32), skip_sum.reshape(shape).astype(F32)


def solution(mesh):
    in_specs = (P("seq", None), P(), P(), P(), P())
    out_specs = (P("seq", None), P("seq", None))
    return jax.shard_map(body, mesh=mesh, in_specs=in_specs, out_specs=out_specs, check_vma=False)
```

```python
import jax
import jax.numpy as jnp
from jax import lax
from jax.experimental import pallas as pl
from jax.experimental.pallas import tpu as pltpu
from jax.sharding import PartitionSpec as P

LAYERS = 6
HALVES = 2
RESIDUES = 512
GROUP = 16
LENGTH = 512
C = 256
PAD = 32
TILE = 256
MESH = pl.DeviceIdType.MESH
BF16 = jnp.bfloat16
F32 = jnp.float32

ALONG_Z = [(dz, dc) for dz in (1, 7, 2, 6, 3, 5, 4, 0) for dc in (0, 1) if (dz, dc) != (0, 0)]
ACROSS = [(dy, dx) for dy in (0, 1, 3, 2) for dx in (1, 3, 2, 0) if (dy, dx) != (0, 0)]


def one_hot(rows, source):
    out = lax.broadcasted_iota(jnp.int32, (rows, rows), 0)
    col = lax.broadcasted_iota(jnp.int32, (rows, rows), 1)
    return jnp.where(col == source(out), 1.0, 0.0).astype(BF16)


def reordered(matrix, rows):
    return jnp.dot(matrix, rows, preferred_element_type=F32)


def kernel(
    signal_hbm,
    conv_hbm,
    bias_ref,
    res_hbm,
    skip_hbm,
    delta_out,
    skip_out,
    signal,
    conv,
    proj,
    swap256,
    split512,
    join512,
    turn512,
    enter512,
    sent_xy,
    sent_z,
    sent_late,
    first_xy,
    first_z,
    next_z,
    next_xy,
    halves,
    late_z,
    late_next,
    late,
    leave,
    passing,
    last,
    cur,
    skip,
    start,
    result,
    x3,
    load_sem,
    weight_sem,
    send_sem,
    recv_sem,
    own_sem,
):
    me = lax.axis_index("seq")
    j, g = lax.rem(me, GROUP), me // GROUP
    z, core = j // 2, lax.rem(j, 2)
    y, x = g // 4, lax.rem(g, 4)
    z_peers = [lax.rem(z + dz, 8) * 2 + lax.rem(core + dc, 2) for dz, dc in ALONG_Z]
    xy_peers = [lax.rem(y + dy, 4) * 4 + lax.rem(x + dx, 4) for dy, dx in ACROSS]

    barrier = pltpu.get_barrier_semaphore()
    for peer in z_peers:
        pl.semaphore_signal(barrier, inc=1, device_id=(g * GROUP + peer,), device_id_type=MESH)
    for peer in xy_peers:
        pl.semaphore_signal(barrier, inc=1, device_id=(peer * GROUP + j,), device_id_type=MESH)

    load = pltpu.make_async_copy(signal_hbm, signal, load_sem)
    load.start()
    weights = [
        pltpu.make_async_copy(conv_hbm, conv, weight_sem.at[0]),
        pltpu.make_async_copy(res_hbm, proj.at[:, :, pl.ds(0, C)], weight_sem.at[1]),
        pltpu.make_async_copy(skip_hbm, proj.at[:, :, pl.ds(C, C)], weight_sem.at[2]),
    ]
    for copy in weights:
        copy.start()
    swap256[...] = one_hot(256, lambda o: (o & 15) * 16 + (o >> 4))
    split512[...] = one_hot(LENGTH, lambda o: (o & 31) * 16 + (o >> 5))
    join512[...] = one_hot(LENGTH, lambda o: (o & 15) * 32 + (o >> 4))
    turn512[...] = one_hot(LENGTH, lambda o: ((o >> 1) & 15) * 32 + (o >> 5) * 2 + (o & 1))
    enter512[...] = one_hot(
        LENGTH,
        lambda o: jnp.where(
            (o & 1) == 0, ((o >> 1) & 15) * 16 + (o >> 5), 256 + (o >> 5) * 16 + ((o >> 1) & 15)
        ),
    )
    cur[pl.ds(0, PAD), :] = jnp.zeros((PAD, C), F32)
    cur[pl.ds(PAD + LENGTH, PAD), :] = jnp.zeros((PAD, C), F32)
    load.wait()
    slab = (GROUP, 16, C)
    sent_xy[...] = signal[0, pl.ds(0, 256), :].astype(BF16).reshape(slab)
    swap = swap256[...]
    sent_z[...] = reordered(swap, signal[1, pl.ds(0, 256), :].astype(BF16)).astype(BF16).reshape(slab)
    for half in range(HALVES):
        rows = reordered(swap, signal[half, pl.ds(256, 256), :].astype(BF16))
        sent_late[:, half] = rows.astype(BF16).reshape(slab)
    pl.semaphore_wait(barrier, 2 * (GROUP - 1))

    started = []

    def send(src, dst, peer, along_z, stage):
        device = g * GROUP + peer if along_z else peer * GROUP + j
        pltpu.make_async_remote_copy(
            src_ref=src,
            dst_ref=dst,
            send_sem=send_sem.at[stage],
            recv_sem=recv_sem.at[stage],
            device_id=(device,),
            device_id_type=MESH,
        ).start()

    def exchange(source, target, along_z, stage):
        mine = j if along_z else g
        for peer in z_peers if along_z else xy_peers:
            send(source.at[peer], target.at[mine], peer, along_z, stage)
        target[mine] = source[mine]
        started.append((source, stage))

    def finish(source, sem):
        part = source.at[pl.ds(0, GROUP - 1)]
        pltpu.make_async_copy(part, part, sem).wait()

    def wait_for(target, stage):
        finish(target, recv_sem.at[stage])

    exchange(sent_xy, first_xy, False, 0)
    exchange(sent_z, first_z, True, 1)
    wait_for(first_xy, 0)
    next_z[...] = reordered(swap256[...], first_xy[...].reshape(256, C)).astype(BF16).reshape(slab)
    exchange(next_z, halves.at[0], True, 2)
    exchange(sent_late, late_z, True, 3)
    wait_for(first_z, 1)
    next_xy[...] = reordered(swap256[...], first_z[...].reshape(256, C)).astype(BF16).reshape(slab)
    exchange(next_xy, halves.at[1], False, 4)

    def layers():
        for layer in range(LAYERS):
            d = 2**layer
            for tap in range(3):
                x3[:, pl.ds(tap * C, C)] = cur[pl.ds(PAD + (tap - 1) * d, LENGTH), :].astype(BF16)
            for tile in range(LENGTH // TILE):
                at = pl.ds(tile * TILE, TILE)
                at_cur = pl.ds(PAD + tile * TILE, TILE)
                pre = jnp.dot(x3[at, :], conv[layer], preferred_element_type=F32)
                pre = pre + bias_ref[pl.ds(layer, 1), :]
                gated = (jnp.tanh(pre[:, :C]) * (0.5 + 0.5 * jnp.tanh(0.5 * pre[:, C:]))).astype(BF16)
                both = jnp.dot(gated, proj[layer], preferred_element_type=F32)
                if layer < LAYERS - 1:
                    cur[at_cur, :] = cur[at_cur, :] + both[:, :C]
                    skip[at, :] = both[:, C:] if layer == 0 else skip[at, :] + both[:, C:]
                else:
                    delta = (cur[at_cur, :] - start[at, :].astype(F32)) + both[:, :C]
                    result[0, at, :] = delta.astype(BF16)
                    result[1, at, :] = (skip[at, :] + both[:, C:]).astype(BF16)

    wide = (GROUP, 32, C)

    def leave_along_z(unit, part, stage):
        rows = reordered(turn512[...], result[part])
        leave[unit] = rows.astype(BF16).reshape(wide)
        exchange(leave.at[unit], passing.at[unit], True, stage)

    own = []

    def last_stage(unit, out, chunk, along_z, arrival, stage):
        wait_for(passing.at[unit], arrival)
        rows = reordered(join512[...], passing[unit].reshape(LENGTH, C))
        last[unit] = rows.astype(BF16).reshape(GROUP, HALVES, 16, C)
        mine = j if along_z else g
        owner = j if along_z else g
        at = pl.ds(pl.multiple_of(chunk * 256 + owner * 16, 16), 16)
        for peer in z_peers if along_z else xy_peers:
            send(last.at[unit, peer], out.at[:, at, :], peer, along_z, stage)
        copy = pltpu.make_async_copy(last.at[unit, mine], out.at[:, at, :], own_sem.at[unit])
        copy.start()
        own.append(copy)
        started.append((last.at[unit], stage))

    for copy in weights:
        copy.wait()
    wait_for(halves.at[0], 2)
    wait_for(halves.at[1], 4)
    rows = reordered(enter512[...], halves[...].reshape(LENGTH, C))
    cur[pl.ds(PAD, LENGTH), :] = rows
    start[...] = rows.astype(BF16)
    layers()
    leave_along_z(0, 0, 6)
    leave_along_z(1, 1, 7)

    wait_for(late_z, 3)
    rows = reordered(split512[...], late_z[...].reshape(LENGTH, C))
    late_next[...] = rows.astype(BF16).reshape(wide)
    exchange(late_next, late, False, 5)
    wait_for(late, 5)
    start[...] = late[...].reshape(LENGTH, C)
    cur[pl.ds(PAD, LENGTH), :] = start[...].astype(F32)
    layers()
    leave[3] = result[1].reshape(wide)
    exchange(leave.at[3], passing.at[3], False, 9)
    leave_along_z(2, 0, 8)

    last_stage(0, delta_out, 0, False, 6, 10)
    last_stage(1, skip_out, 0, False, 7, 11)
    last_stage(3, skip_out, 1, True, 9, 13)
    last_stage(2, delta_out, 1, False, 8, 12)

    for unit, stage in ((0, 10), (1, 11), (3, 13), (2, 12)):
        wait_for(last.at[unit], stage)
    for copy in own:
        copy.wait()
    for source, stage in started:
        finish(source, send_sem.at[stage])


def finish_kernel(signal_ref, delta_ref, skip_in_ref, features_ref, skip_ref):
    features_ref[...] = signal_ref[...] + delta_ref[...].astype(F32)
    chunk = lax.rem(pl.program_id(0), 2)

    @pl.when(chunk == 0)
    def _():
        skip_ref[...] = skip_in_ref[...].astype(F32)

    @pl.when(chunk == 1)
    def _():
        swap = one_hot(256, lambda o: (o & 15) * 16 + (o >> 4))
        skip_ref[...] = reordered(swap, skip_in_ref[...])


def body(signal, conv_weight, conv_bias, res_weight, skip_weight):
    any_space = pl.BlockSpec(memory_space=pl.ANY)

    def vmem(*shape, dtype=BF16):
        return pltpu.VMEM(shape, dtype)

    delta, skip_sum = pl.pallas_call(
        kernel,
        out_shape=[jax.ShapeDtypeStruct((HALVES, RESIDUES, C), BF16)] * 2,
        in_specs=[any_space, any_space, pl.BlockSpec(memory_space=pltpu.VMEM), any_space, any_space],
        out_specs=[any_space, any_space],
        scratch_shapes=[
            vmem(HALVES, RESIDUES, C, dtype=F32),
            vmem(LAYERS, 3 * C, 2 * C),
            vmem(LAYERS, C, 2 * C),
            vmem(256, 256),
            vmem(LENGTH, LENGTH),
            vmem(LENGTH, LENGTH),
            vmem(LENGTH, LENGTH),
            vmem(LENGTH, LENGTH),
            vmem(GROUP, 16, C),
            vmem(GROUP, 16, C),
            vmem(GROUP, HALVES, 16, C),
            vmem(GROUP, 16, C),
            vmem(GROUP, 16, C),
            vmem(GROUP, 16, C),
            vmem(GROUP, 16, C),
            vmem(2, GROUP, 16, C),
            vmem(GROUP, HALVES, 16, C),
            vmem(GROUP, 32, C),
            vmem(GROUP, 32, C),
            vmem(4, GROUP, 32, C),
            vmem(4, GROUP, 32, C),
            vmem(4, GROUP, HALVES, 16, C),
            vmem(LENGTH + 2 * PAD, C, dtype=F32),
            vmem(LENGTH, C, dtype=F32),
            vmem(LENGTH, C),
            vmem(2, LENGTH, C),
            vmem(LENGTH, 3 * C),
            pltpu.SemaphoreType.DMA,
            pltpu.SemaphoreType.DMA((3,)),
            pltpu.SemaphoreType.DMA((14,)),
            pltpu.SemaphoreType.DMA((14,)),
            pltpu.SemaphoreType.DMA((4,)),
        ],
        compiler_params=pltpu.CompilerParams(
            collective_id=0, has_side_effects=True, vmem_limit_bytes=60 * 2**20
        ),
    )(
        signal.reshape(HALVES, RESIDUES, C),
        conv_weight,
        conv_bias,
        res_weight,
        skip_weight,
    )
    block = pl.BlockSpec((256, C), lambda i: (i, 0))
    shape = signal.shape
    return pl.pallas_call(
        finish_kernel,
        grid=(shape[0] // 256,),
        out_shape=[jax.ShapeDtypeStruct(shape, F32)] * 2,
        in_specs=[block, block, block],
        out_specs=[block, block],
    )(signal, delta.reshape(shape), skip_sum.reshape(shape))


def solution(mesh):
    in_specs = (P("seq", None), P(), P(), P(), P())
    out_specs = (P("seq", None), P("seq", None))
    return jax.shard_map(body, mesh=mesh, in_specs=in_specs, out_specs=out_specs, check_vma=False)
```

```python
import jax
import jax.numpy as jnp
from jax import lax
from jax.experimental import pallas as pl
from jax.experimental.pallas import tpu as pltpu
from jax.sharding import PartitionSpec as P

LAYERS = 6
HALVES = 2
RESIDUES = 512
GROUP = 16
LENGTH = 512
C = 256
PAD = 32
MESH = pl.DeviceIdType.MESH
BF16 = jnp.bfloat16
F32 = jnp.float32

ALONG_Z = [(dz, dc) for dz in (1, 7, 2, 6, 3, 5, 4, 0) for dc in (0, 1) if (dz, dc) != (0, 0)]
ACROSS = [(dy, dx) for dy in (0, 1, 3, 2) for dx in (1, 3, 2, 0) if (dy, dx) != (0, 0)]


def one_hot(rows, source):
    out = lax.broadcasted_iota(jnp.int32, (rows, rows), 0)
    col = lax.broadcasted_iota(jnp.int32, (rows, rows), 1)
    return jnp.where(col == source(out), 1.0, 0.0).astype(BF16)


def reordered(matrix, rows):
    return jnp.dot(matrix, rows, preferred_element_type=F32)


def kernel(
    signal_hbm,
    conv_hbm,
    bias_ref,
    res_hbm,
    skip_hbm,
    delta_out,
    skip_out,
    signal,
    conv,
    proj,
    swap256,
    split512,
    join512,
    turn512,
    enter512,
    sent_xy,
    sent_z,
    sent_late,
    first_xy,
    first_z,
    next_z,
    next_xy,
    halves,
    late_z,
    late_next,
    late,
    leave,
    passing,
    last,
    cur,
    skip,
    start,
    result,
    x3,
    load_sem,
    weight_sem,
    send_sem,
    recv_sem,
    own_sem,
):
    me = lax.axis_index("seq")
    j, g = lax.rem(me, GROUP), me // GROUP
    z, core = j // 2, lax.rem(j, 2)
    y, x = g // 4, lax.rem(g, 4)
    z_peers = [lax.rem(z + dz, 8) * 2 + lax.rem(core + dc, 2) for dz, dc in ALONG_Z]
    xy_peers = [lax.rem(y + dy, 4) * 4 + lax.rem(x + dx, 4) for dy, dx in ACROSS]

    barrier = pltpu.get_barrier_semaphore()
    for peer in z_peers:
        pl.semaphore_signal(barrier, inc=1, device_id=(g * GROUP + peer,), device_id_type=MESH)
    for peer in xy_peers:
        pl.semaphore_signal(barrier, inc=1, device_id=(peer * GROUP + j,), device_id_type=MESH)

    load = pltpu.make_async_copy(signal_hbm, signal, load_sem)
    load.start()
    weights = [
        pltpu.make_async_copy(conv_hbm, conv, weight_sem.at[0]),
        pltpu.make_async_copy(res_hbm, proj.at[:, :, pl.ds(0, C)], weight_sem.at[1]),
        pltpu.make_async_copy(skip_hbm, proj.at[:, :, pl.ds(C, C)], weight_sem.at[2]),
    ]
    for copy in weights:
        copy.start()
    swap256[...] = one_hot(256, lambda o: (o & 15) * 16 + (o >> 4))
    split512[...] = one_hot(LENGTH, lambda o: (o & 31) * 16 + (o >> 5))
    join512[...] = one_hot(LENGTH, lambda o: (o & 15) * 32 + (o >> 4))
    turn512[...] = one_hot(LENGTH, lambda o: ((o >> 1) & 15) * 32 + (o >> 5) * 2 + (o & 1))
    enter512[...] = one_hot(
        LENGTH,
        lambda o: jnp.where(
            (o & 1) == 0, ((o >> 1) & 15) * 16 + (o >> 5), 256 + (o >> 5) * 16 + ((o >> 1) & 15)
        ),
    )
    cur[pl.ds(0, PAD), :] = jnp.zeros((PAD, C), F32)
    cur[pl.ds(PAD + LENGTH, PAD), :] = jnp.zeros((PAD, C), F32)
    load.wait()
    slab = (GROUP, 16, C)
    sent_xy[...] = signal[0, pl.ds(0, 256), :].astype(BF16).reshape(slab)
    swap = swap256[...]
    sent_z[...] = reordered(swap, signal[1, pl.ds(0, 256), :].astype(BF16)).astype(BF16).reshape(slab)
    for half in range(HALVES):
        rows = reordered(swap, signal[half, pl.ds(256, 256), :].astype(BF16))
        sent_late[:, half] = rows.astype(BF16).reshape(slab)
    for copy in weights:
        copy.wait()
    for layer in range(LAYERS):
        conv[layer, :, pl.ds(C, C)] = conv[layer, :, pl.ds(C, C)] * jnp.asarray(0.5, BF16)
        proj[layer] = proj[layer] * jnp.asarray(0.5, BF16)
    pl.semaphore_wait(barrier, 2 * (GROUP - 1))

    started = {}

    def send(src, dst, peer, along_z, stage):
        device = g * GROUP + peer if along_z else peer * GROUP + j
        pltpu.make_async_remote_copy(
            src_ref=src,
            dst_ref=dst,
            send_sem=send_sem.at[stage],
            recv_sem=recv_sem.at[stage],
            device_id=(device,),
            device_id_type=MESH,
        ).start()

    def exchange(source, target, along_z, stage):
        mine = j if along_z else g
        for peer in z_peers if along_z else xy_peers:
            send(source.at[peer], target.at[mine], peer, along_z, stage)
        target[mine] = source[mine]
        started[stage] = source

    def finish(source, sem):
        part = source.at[pl.ds(0, GROUP - 1)]
        pltpu.make_async_copy(part, part, sem).wait()

    def wait_for(target, stage):
        finish(target, recv_sem.at[stage])

    exchange(sent_xy, first_xy, False, 0)
    exchange(sent_z, first_z, True, 1)
    wait_for(first_xy, 0)
    next_z[...] = reordered(swap256[...], first_xy[...].reshape(256, C)).astype(BF16).reshape(slab)
    exchange(next_z, halves.at[0], True, 2)
    exchange(sent_late, late_z, True, 3)
    wait_for(first_z, 1)
    next_xy[...] = reordered(swap256[...], first_z[...].reshape(256, C)).astype(BF16).reshape(slab)
    exchange(next_xy, halves.at[1], False, 4)

    def layers():
        for layer in range(LAYERS):
            d = 2**layer
            for tap in range(3):
                x3[:, pl.ds(tap * C, C)] = cur[pl.ds(PAD + (tap - 1) * d, LENGTH), :].astype(BF16)
            pre = jnp.dot(x3[...], conv[layer], preferred_element_type=F32)
            filtered = jnp.tanh(pre[:, :C] + bias_ref[pl.ds(layer, 1), pl.ds(0, C)])
            gate = jnp.tanh(pre[:, C:] + 0.5 * bias_ref[pl.ds(layer, 1), pl.ds(C, C)])
            twice_gated = (filtered + filtered * gate).astype(BF16)
            both = jnp.dot(twice_gated, proj[layer], preferred_element_type=F32)
            at_cur = pl.ds(PAD, LENGTH)
            if layer < LAYERS - 1:
                cur[at_cur, :] = cur[at_cur, :] + both[:, :C]
                skip[...] = both[:, C:] if layer == 0 else skip[...] + both[:, C:]
            else:
                delta = (cur[at_cur, :] - start[...].astype(F32)) + both[:, :C]
                result[0] = delta.astype(BF16)
                result[1] = (skip[...] + both[:, C:]).astype(BF16)

    wide = (GROUP, 32, C)

    def leave_along_z(unit, part, stage):
        rows = reordered(turn512[...], result[part])
        leave[unit] = rows.astype(BF16).reshape(wide)
        exchange(leave.at[unit], passing.at[unit], True, stage)

    own = []

    def last_stage(unit, out, chunk, along_z, arrival, stage):
        wait_for(passing.at[unit], arrival)
        rows = reordered(join512[...], passing[unit].reshape(LENGTH, C))
        last[unit] = rows.astype(BF16).reshape(GROUP, HALVES, 16, C)
        mine = j if along_z else g
        owner = j if along_z else g
        at = pl.ds(pl.multiple_of(chunk * 256 + owner * 16, 16), 16)
        for peer in z_peers if along_z else xy_peers:
            send(last.at[unit, peer], out.at[:, at, :], peer, along_z, stage)
        copy = pltpu.make_async_copy(last.at[unit, mine], out.at[:, at, :], own_sem.at[unit])
        copy.start()
        own.append(copy)
        started[stage] = last.at[unit]

    wait_for(halves.at[0], 2)
    wait_for(halves.at[1], 4)
    rows = reordered(enter512[...], halves[...].reshape(LENGTH, C))
    cur[pl.ds(PAD, LENGTH), :] = rows
    start[...] = rows.astype(BF16)
    layers()
    leave_along_z(0, 0, 6)

    wait_for(late_z, 3)
    rows = reordered(split512[...], late_z[...].reshape(LENGTH, C))
    late_next[...] = rows.astype(BF16).reshape(wide)
    exchange(late_next, late, False, 5)
    leave_along_z(1, 1, 7)
    wait_for(late, 5)
    start[...] = late[...].reshape(LENGTH, C)
    cur[pl.ds(PAD, LENGTH), :] = start[...].astype(F32)
    layers()
    leave[3] = result[1].reshape(wide)
    exchange(leave.at[3], passing.at[3], False, 9)
    leave_along_z(2, 0, 8)

    last_stage(0, delta_out, 0, False, 6, 10)
    last_stage(1, skip_out, 0, False, 7, 11)
    finish(leave.at[2], send_sem.at[8])
    del started[8]
    last_stage(3, skip_out, 1, True, 9, 13)
    last_stage(2, delta_out, 1, False, 8, 12)

    for unit, stage in ((0, 10), (1, 11), (3, 13), (2, 12)):
        wait_for(last.at[unit], stage)
    for copy in own:
        copy.wait()
    for stage, source in started.items():
        finish(source, send_sem.at[stage])


def finish_kernel(signal_ref, delta_ref, skip_in_ref, features_ref, skip_ref):
    features_ref[...] = signal_ref[...] + delta_ref[...].astype(F32)
    first, second = pl.ds(0, 256), pl.ds(256, 256)
    skip_ref[first, :] = skip_in_ref[first, :].astype(F32)
    swap = one_hot(256, lambda o: (o & 15) * 16 + (o >> 4))
    skip_ref[second, :] = reordered(swap, skip_in_ref[second, :])


def body(signal, conv_weight, conv_bias, res_weight, skip_weight):
    any_space = pl.BlockSpec(memory_space=pl.ANY)

    def vmem(*shape, dtype=BF16):
        return pltpu.VMEM(shape, dtype)

    delta, skip_sum = pl.pallas_call(
        kernel,
        out_shape=[jax.ShapeDtypeStruct((HALVES, RESIDUES, C), BF16)] * 2,
        in_specs=[any_space, any_space, pl.BlockSpec(memory_space=pltpu.VMEM), any_space, any_space],
        out_specs=[any_space, any_space],
        scratch_shapes=[
            vmem(HALVES, RESIDUES, C, dtype=F32),
            vmem(LAYERS, 3 * C, 2 * C),
            vmem(LAYERS, C, 2 * C),
            vmem(256, 256),
            vmem(LENGTH, LENGTH),
            vmem(LENGTH, LENGTH),
            vmem(LENGTH, LENGTH),
            vmem(LENGTH, LENGTH),
            vmem(GROUP, 16, C),
            vmem(GROUP, 16, C),
            vmem(GROUP, HALVES, 16, C),
            vmem(GROUP, 16, C),
            vmem(GROUP, 16, C),
            vmem(GROUP, 16, C),
            vmem(GROUP, 16, C),
            vmem(2, GROUP, 16, C),
            vmem(GROUP, HALVES, 16, C),
            vmem(GROUP, 32, C),
            vmem(GROUP, 32, C),
            vmem(4, GROUP, 32, C),
            vmem(4, GROUP, 32, C),
            vmem(4, GROUP, HALVES, 16, C),
            vmem(LENGTH + 2 * PAD, C, dtype=F32),
            vmem(LENGTH, C, dtype=F32),
            vmem(LENGTH, C),
            vmem(2, LENGTH, C),
            vmem(LENGTH, 3 * C),
            pltpu.SemaphoreType.DMA,
            pltpu.SemaphoreType.DMA((3,)),
            pltpu.SemaphoreType.DMA((14,)),
            pltpu.SemaphoreType.DMA((14,)),
            pltpu.SemaphoreType.DMA((4,)),
        ],
        compiler_params=pltpu.CompilerParams(
            collective_id=0, has_side_effects=True, vmem_limit_bytes=60 * 2**20
        ),
    )(
        signal.reshape(HALVES, RESIDUES, C),
        conv_weight,
        conv_bias,
        res_weight,
        skip_weight,
    )
    block = pl.BlockSpec((RESIDUES, C), lambda i: (i, 0))
    shape = signal.shape
    return pl.pallas_call(
        finish_kernel,
        grid=(HALVES,),
        out_shape=[jax.ShapeDtypeStruct(shape, F32)] * 2,
        in_specs=[block, block, block],
        out_specs=[block, block],
    )(signal, delta.reshape(shape), skip_sum.reshape(shape))


def solution(mesh):
    in_specs = (P("seq", None), P(), P(), P(), P())
    out_specs = (P("seq", None), P("seq", None))
    return jax.shard_map(body, mesh=mesh, in_specs=in_specs, out_specs=out_specs, check_vma=False)
```

```python
import jax
import jax.numpy as jnp
from jax import lax
from jax.experimental import pallas as pl
from jax.experimental.pallas import tpu as pltpu
from jax.sharding import PartitionSpec as P

LAYERS = 6
HALVES = 2
RESIDUES = 512
GROUP = 16
LENGTH = 512
C = 256
PAD = 32
MESH = pl.DeviceIdType.MESH
BF16 = jnp.bfloat16
F32 = jnp.float32

ALONG_Z = [(dz, dc) for dz in (1, 7, 2, 6, 3, 5, 4, 0) for dc in (0, 1) if (dz, dc) != (0, 0)]
ACROSS = [(dy, dx) for dy in (0, 1, 3, 2) for dx in (1, 3, 2, 0) if (dy, dx) != (0, 0)]


def one_hot(rows, source):
    out = lax.broadcasted_iota(jnp.int32, (rows, rows), 0)
    col = lax.broadcasted_iota(jnp.int32, (rows, rows), 1)
    return jnp.where(col == source(out), 1.0, 0.0).astype(BF16)


def reordered(matrix, rows):
    return jnp.dot(matrix, rows, preferred_element_type=F32)


def kernel(
    signal_hbm,
    conv_hbm,
    bias_ref,
    res_hbm,
    skip_hbm,
    delta_out,
    skip_out,
    signal,
    conv,
    res_proj,
    skip_proj,
    swap256,
    split512,
    join512,
    turn512,
    enter512,
    sent_xy,
    sent_z,
    sent_late,
    first_xy,
    first_z,
    next_z,
    next_xy,
    halves,
    late_z,
    late_next,
    late,
    leave,
    passing,
    last,
    cur,
    all_gated,
    start,
    result,
    x3,
    load_sem,
    weight_sem,
    send_sem,
    recv_sem,
    own_sem,
):
    me = lax.axis_index("seq")
    j, g = lax.rem(me, GROUP), me // GROUP
    z, core = j // 2, lax.rem(j, 2)
    y, x = g // 4, lax.rem(g, 4)
    z_peers = [lax.rem(z + dz, 8) * 2 + lax.rem(core + dc, 2) for dz, dc in ALONG_Z]
    xy_peers = [lax.rem(y + dy, 4) * 4 + lax.rem(x + dx, 4) for dy, dx in ACROSS]

    barrier = pltpu.get_barrier_semaphore()
    for peer in z_peers:
        pl.semaphore_signal(barrier, inc=1, device_id=(g * GROUP + peer,), device_id_type=MESH)
    for peer in xy_peers:
        pl.semaphore_signal(barrier, inc=1, device_id=(peer * GROUP + j,), device_id_type=MESH)

    load = pltpu.make_async_copy(signal_hbm, signal, load_sem)
    load.start()
    weights = [
        pltpu.make_async_copy(conv_hbm, conv, weight_sem.at[0]),
        pltpu.make_async_copy(res_hbm, res_proj, weight_sem.at[1]),
        pltpu.make_async_copy(skip_hbm, skip_proj, weight_sem.at[2]),
    ]
    for copy in weights:
        copy.start()
    swap256[...] = one_hot(256, lambda o: (o & 15) * 16 + (o >> 4))
    split512[...] = one_hot(LENGTH, lambda o: (o & 31) * 16 + (o >> 5))
    join512[...] = one_hot(LENGTH, lambda o: (o & 15) * 32 + (o >> 4))
    turn512[...] = one_hot(LENGTH, lambda o: ((o >> 1) & 15) * 32 + (o >> 5) * 2 + (o & 1))
    enter512[...] = one_hot(
        LENGTH,
        lambda o: jnp.where(
            (o & 1) == 0, ((o >> 1) & 15) * 16 + (o >> 5), 256 + (o >> 5) * 16 + ((o >> 1) & 15)
        ),
    )
    cur[pl.ds(0, PAD), :] = jnp.zeros((PAD, C), F32)
    cur[pl.ds(PAD + LENGTH, PAD), :] = jnp.zeros((PAD, C), F32)
    load.wait()
    slab = (GROUP, 16, C)
    sent_xy[...] = signal[0, pl.ds(0, 256), :].astype(BF16).reshape(slab)
    swap = swap256[...]
    sent_z[...] = reordered(swap, signal[1, pl.ds(0, 256), :].astype(BF16)).astype(BF16).reshape(slab)
    for half in range(HALVES):
        rows = reordered(swap, signal[half, pl.ds(256, 256), :].astype(BF16))
        sent_late[:, half] = rows.astype(BF16).reshape(slab)
    for copy in weights:
        copy.wait()
    for layer in range(LAYERS):
        conv[layer, :, pl.ds(C, C)] = conv[layer, :, pl.ds(C, C)] * jnp.asarray(0.5, BF16)
        res_proj[layer] = res_proj[layer] * jnp.asarray(0.5, BF16)
        at = pl.ds(layer * C, C)
        skip_proj[at, :] = skip_proj[at, :] * jnp.asarray(0.5, BF16)
    pl.semaphore_wait(barrier, 2 * (GROUP - 1))

    started = {}

    def send(src, dst, peer, along_z, stage):
        device = g * GROUP + peer if along_z else peer * GROUP + j
        pltpu.make_async_remote_copy(
            src_ref=src,
            dst_ref=dst,
            send_sem=send_sem.at[stage],
            recv_sem=recv_sem.at[stage],
            device_id=(device,),
            device_id_type=MESH,
        ).start()

    def exchange(source, target, along_z, stage):
        mine = j if along_z else g
        for peer in z_peers if along_z else xy_peers:
            send(source.at[peer], target.at[mine], peer, along_z, stage)
        target[mine] = source[mine]
        started[stage] = source

    def finish(source, sem):
        part = source.at[pl.ds(0, GROUP - 1)]
        pltpu.make_async_copy(part, part, sem).wait()

    def wait_for(target, stage):
        finish(target, recv_sem.at[stage])

    exchange(sent_xy, first_xy, False, 0)
    exchange(sent_z, first_z, True, 1)
    wait_for(first_xy, 0)
    next_z[...] = reordered(swap256[...], first_xy[...].reshape(256, C)).astype(BF16).reshape(slab)
    exchange(next_z, halves.at[0], True, 2)
    wait_for(first_z, 1)
    next_xy[...] = reordered(swap256[...], first_z[...].reshape(256, C)).astype(BF16).reshape(slab)
    exchange(next_xy, halves.at[1], False, 4)
    finish(next_z, send_sem.at[2])
    del started[2]
    exchange(sent_late, late_z, True, 3)

    def layers():
        for layer in range(LAYERS):
            d = 2**layer
            for tap in range(3):
                x3[:, pl.ds(tap * C, C)] = cur[pl.ds(PAD + (tap - 1) * d, LENGTH), :].astype(BF16)
            pre = jnp.dot(x3[...], conv[layer], preferred_element_type=F32)
            filtered = jnp.tanh(pre[:, :C] + bias_ref[pl.ds(layer, 1), pl.ds(0, C)])
            gate = jnp.tanh(pre[:, C:] + 0.5 * bias_ref[pl.ds(layer, 1), pl.ds(C, C)])
            twice_gated = (filtered + filtered * gate).astype(BF16)
            all_gated[:, pl.ds(layer * C, C)] = twice_gated
            added = jnp.dot(twice_gated, res_proj[layer], preferred_element_type=F32)
            at_cur = pl.ds(PAD, LENGTH)
            if layer < LAYERS - 1:
                cur[at_cur, :] = cur[at_cur, :] + added
            else:
                result[0] = ((cur[at_cur, :] - start[...].astype(F32)) + added).astype(BF16)

    def skip_sums():
        sums = jnp.dot(all_gated[...], skip_proj[...], preferred_element_type=F32)
        result[1] = sums.astype(BF16)

    wide = (GROUP, 32, C)

    def leave_along_z(unit, part, stage):
        rows = reordered(turn512[...], result[part])
        leave[unit] = rows.astype(BF16).reshape(wide)
        exchange(leave.at[unit], passing.at[unit], True, stage)

    own = []

    def last_stage(unit, out, chunk, along_z, arrival, stage):
        wait_for(passing.at[unit], arrival)
        rows = reordered(join512[...], passing[unit].reshape(LENGTH, C))
        last[unit] = rows.astype(BF16).reshape(GROUP, HALVES, 16, C)
        mine = j if along_z else g
        owner = j if along_z else g
        at = pl.ds(pl.multiple_of(chunk * 256 + owner * 16, 16), 16)
        for peer in z_peers if along_z else xy_peers:
            send(last.at[unit, peer], out.at[:, at, :], peer, along_z, stage)
        copy = pltpu.make_async_copy(last.at[unit, mine], out.at[:, at, :], own_sem.at[unit])
        copy.start()
        own.append(copy)
        started[stage] = last.at[unit]

    wait_for(halves.at[0], 2)
    wait_for(halves.at[1], 4)
    rows = reordered(enter512[...], halves[...].reshape(LENGTH, C))
    cur[pl.ds(PAD, LENGTH), :] = rows
    start[...] = rows.astype(BF16)
    layers()
    leave_along_z(0, 0, 6)
    skip_sums()
    leave_along_z(1, 1, 7)

    wait_for(late_z, 3)
    rows = reordered(split512[...], late_z[...].reshape(LENGTH, C))
    late_next[...] = rows.astype(BF16).reshape(wide)
    exchange(late_next, late, False, 5)
    wait_for(late, 5)
    start[...] = late[...].reshape(LENGTH, C)
    cur[pl.ds(PAD, LENGTH), :] = start[...].astype(F32)
    layers()
    leave[2] = result[0].reshape(wide)
    exchange(leave.at[2], passing.at[2], False, 8)
    skip_sums()
    leave_along_z(3, 1, 9)

    last_stage(0, delta_out, 0, False, 6, 10)
    last_stage(1, skip_out, 0, False, 7, 11)
    finish(leave.at[3], send_sem.at[9])
    del started[9]
    last_stage(2, delta_out, 1, True, 8, 12)
    last_stage(3, skip_out, 1, False, 9, 13)

    for unit, stage in ((0, 10), (1, 11), (2, 12), (3, 13)):
        wait_for(last.at[unit], stage)
    for copy in own:
        copy.wait()
    for stage, source in started.items():
        finish(source, send_sem.at[stage])


def finish_kernel(signal_ref, delta_ref, skip_in_ref, features_ref, skip_ref):
    skip_ref[...] = skip_in_ref[...].astype(F32)
    first, second = pl.ds(0, 256), pl.ds(256, 256)
    features_ref[first, :] = signal_ref[first, :] + delta_ref[first, :].astype(F32)
    swap = one_hot(256, lambda o: (o & 15) * 16 + (o >> 4))
    features_ref[second, :] = signal_ref[second, :] + reordered(swap, delta_ref[second, :])


def body(signal, conv_weight, conv_bias, res_weight, skip_weight):
    any_space = pl.BlockSpec(memory_space=pl.ANY)

    def vmem(*shape, dtype=BF16):
        return pltpu.VMEM(shape, dtype)

    delta, skip_sum = pl.pallas_call(
        kernel,
        out_shape=[jax.ShapeDtypeStruct((HALVES, RESIDUES, C), BF16)] * 2,
        in_specs=[any_space, any_space, pl.BlockSpec(memory_space=pltpu.VMEM), any_space, any_space],
        out_specs=[any_space, any_space],
        scratch_shapes=[
            vmem(HALVES, RESIDUES, C, dtype=F32),
            vmem(LAYERS, 3 * C, 2 * C),
            vmem(LAYERS, C, C),
            vmem(LAYERS * C, C),
            vmem(256, 256),
            vmem(LENGTH, LENGTH),
            vmem(LENGTH, LENGTH),
            vmem(LENGTH, LENGTH),
            vmem(LENGTH, LENGTH),
            vmem(GROUP, 16, C),
            vmem(GROUP, 16, C),
            vmem(GROUP, HALVES, 16, C),
            vmem(GROUP, 16, C),
            vmem(GROUP, 16, C),
            vmem(GROUP, 16, C),
            vmem(GROUP, 16, C),
            vmem(2, GROUP, 16, C),
            vmem(GROUP, HALVES, 16, C),
            vmem(GROUP, 32, C),
            vmem(GROUP, 32, C),
            vmem(4, GROUP, 32, C),
            vmem(4, GROUP, 32, C),
            vmem(4, GROUP, HALVES, 16, C),
            vmem(LENGTH + 2 * PAD, C, dtype=F32),
            vmem(LENGTH, LAYERS * C),
            vmem(LENGTH, C),
            vmem(2, LENGTH, C),
            vmem(LENGTH, 3 * C),
            pltpu.SemaphoreType.DMA,
            pltpu.SemaphoreType.DMA((3,)),
            pltpu.SemaphoreType.DMA((14,)),
            pltpu.SemaphoreType.DMA((14,)),
            pltpu.SemaphoreType.DMA((4,)),
        ],
        compiler_params=pltpu.CompilerParams(
            collective_id=0, has_side_effects=True, vmem_limit_bytes=60 * 2**20
        ),
    )(
        signal.reshape(HALVES, RESIDUES, C),
        conv_weight,
        conv_bias,
        res_weight,
        skip_weight.reshape(LAYERS * C, C),
    )
    block = pl.BlockSpec((RESIDUES, C), lambda i: (i, 0))
    shape = signal.shape
    return pl.pallas_call(
        finish_kernel,
        grid=(HALVES,),
        out_shape=[jax.ShapeDtypeStruct(shape, F32)] * 2,
        in_specs=[block, block, block],
        out_specs=[block, block],
    )(signal, delta.reshape(shape), skip_sum.reshape(shape))


def solution(mesh):
    in_specs = (P("seq", None), P(), P(), P(), P())
    out_specs = (P("seq", None), P("seq", None))
    return jax.shard_map(body, mesh=mesh, in_specs=in_specs, out_specs=out_specs, check_vma=False)
```

```python
import jax
import jax.numpy as jnp
from jax import lax
from jax.experimental import pallas as pl
from jax.experimental.pallas import tpu as pltpu
from jax.sharding import PartitionSpec as P

LAYERS = 6
HALVES = 2
RESIDUES = 512
GROUP = 16
LENGTH = 512
C = 256
PAD = 32
MESH = pl.DeviceIdType.MESH
BF16 = jnp.bfloat16
F32 = jnp.float32

ALONG_Z = [(dz, dc) for dz in (1, 7, 2, 6, 3, 5, 4, 0) for dc in (0, 1) if (dz, dc) != (0, 0)]
ACROSS = [(dy, dx) for dy in (0, 1, 3, 2) for dx in (1, 3, 2, 0) if (dy, dx) != (0, 0)]


def one_hot(rows, source):
    out = lax.broadcasted_iota(jnp.int32, (rows, rows), 0)
    col = lax.broadcasted_iota(jnp.int32, (rows, rows), 1)
    return jnp.where(col == source(out), 1.0, 0.0).astype(BF16)


def reordered(matrix, rows):
    return jnp.dot(matrix, rows, preferred_element_type=F32)


def kernel(
    signal_hbm,
    conv_hbm,
    bias_ref,
    res_hbm,
    skip_hbm,
    delta_out,
    skip_out,
    signal,
    conv,
    res_proj,
    skip_proj,
    swap256,
    split512,
    join512,
    turn512,
    enter512,
    sent_xy,
    sent_z,
    sent_late,
    first_xy,
    first_z,
    next_z,
    next_xy,
    halves,
    late_first,
    late_next,
    late,
    leave,
    passing,
    last,
    cur,
    all_gated,
    start,
    result,
    x3,
    load_sem,
    weight_sem,
    send_sem,
    recv_sem,
    own_sem,
):
    me = lax.axis_index("seq")
    j, g = lax.rem(me, GROUP), me // GROUP
    z, core = j // 2, lax.rem(j, 2)
    y, x = g // 4, lax.rem(g, 4)
    z_peers = [lax.rem(z + dz, 8) * 2 + lax.rem(core + dc, 2) for dz, dc in ALONG_Z]
    xy_peers = [lax.rem(y + dy, 4) * 4 + lax.rem(x + dx, 4) for dy, dx in ACROSS]

    barrier = pltpu.get_barrier_semaphore()
    for peer in z_peers:
        pl.semaphore_signal(barrier, inc=1, device_id=(g * GROUP + peer,), device_id_type=MESH)
    for peer in xy_peers:
        pl.semaphore_signal(barrier, inc=1, device_id=(peer * GROUP + j,), device_id_type=MESH)

    load = pltpu.make_async_copy(signal_hbm, signal, load_sem)
    load.start()
    weights = [
        pltpu.make_async_copy(conv_hbm, conv, weight_sem.at[0]),
        pltpu.make_async_copy(res_hbm, res_proj, weight_sem.at[1]),
        pltpu.make_async_copy(skip_hbm, skip_proj, weight_sem.at[2]),
    ]
    for copy in weights:
        copy.start()
    swap256[...] = one_hot(256, lambda o: (o & 15) * 16 + (o >> 4))
    split512[...] = one_hot(LENGTH, lambda o: (o & 31) * 16 + (o >> 5))
    join512[...] = one_hot(LENGTH, lambda o: (o & 15) * 32 + (o >> 4))
    turn512[...] = one_hot(LENGTH, lambda o: ((o >> 1) & 15) * 32 + (o >> 5) * 2 + (o & 1))
    enter512[...] = one_hot(
        LENGTH,
        lambda o: jnp.where(
            (o & 1) == 0, ((o >> 1) & 15) * 16 + (o >> 5), 256 + (o >> 5) * 16 + ((o >> 1) & 15)
        ),
    )
    cur[pl.ds(0, PAD), :] = jnp.zeros((PAD, C), F32)
    cur[pl.ds(PAD + LENGTH, PAD), :] = jnp.zeros((PAD, C), F32)
    load.wait()
    slab = (GROUP, 16, C)
    sent_xy[...] = signal[0, pl.ds(0, 256), :].astype(BF16).reshape(slab)
    sent_z[...] = reordered(swap256[...], signal[1, pl.ds(0, 256), :].astype(BF16)).astype(BF16).reshape(slab)
    for half in range(HALVES):
        sent_late[:, half] = signal[half, pl.ds(256, 256), :].astype(BF16).reshape(slab)
    for copy in weights:
        copy.wait()
    for layer in range(LAYERS):
        conv[layer, :, pl.ds(C, C)] = conv[layer, :, pl.ds(C, C)] * jnp.asarray(0.5, BF16)
        res_proj[layer] = res_proj[layer] * jnp.asarray(0.5, BF16)
        at = pl.ds(layer * C, C)
        skip_proj[at, :] = skip_proj[at, :] * jnp.asarray(0.5, BF16)
    pl.semaphore_wait(barrier, 2 * (GROUP - 1))

    started = {}

    def send(src, dst, peer, along_z, stage):
        device = g * GROUP + peer if along_z else peer * GROUP + j
        pltpu.make_async_remote_copy(
            src_ref=src,
            dst_ref=dst,
            send_sem=send_sem.at[stage],
            recv_sem=recv_sem.at[stage],
            device_id=(device,),
            device_id_type=MESH,
        ).start()

    def exchange(source, target, along_z, stage):
        mine = j if along_z else g
        for peer in z_peers if along_z else xy_peers:
            send(source.at[peer], target.at[mine], peer, along_z, stage)
        target[mine] = source[mine]
        started[stage] = source

    def finish(source, sem):
        part = source.at[pl.ds(0, GROUP - 1)]
        pltpu.make_async_copy(part, part, sem).wait()

    def wait_for(target, stage):
        finish(target, recv_sem.at[stage])

    exchange(sent_xy, first_xy, False, 0)
    exchange(sent_z, first_z, True, 1)
    exchange(sent_late, late_first, False, 3)
    wait_for(first_xy, 0)
    next_z[...] = reordered(swap256[...], first_xy[...].reshape(256, C)).astype(BF16).reshape(slab)
    exchange(next_z, halves.at[0], True, 2)
    wait_for(first_z, 1)
    next_xy[...] = reordered(swap256[...], first_z[...].reshape(256, C)).astype(BF16).reshape(slab)
    exchange(next_xy, halves.at[1], False, 4)
    wait_for(late_first, 3)
    rows = reordered(split512[...], late_first[...].reshape(LENGTH, C))
    late_next[...] = rows.astype(BF16).reshape(GROUP, 32, C)
    exchange(late_next, late, True, 5)

    def layers():
        for layer in range(LAYERS):
            d = 2**layer
            for tap in range(3):
                x3[:, pl.ds(tap * C, C)] = cur[pl.ds(PAD + (tap - 1) * d, LENGTH), :].astype(BF16)
            pre = jnp.dot(x3[...], conv[layer], preferred_element_type=F32)
            filtered = jnp.tanh(pre[:, :C] + bias_ref[pl.ds(layer, 1), pl.ds(0, C)])
            gate = jnp.tanh(pre[:, C:] + 0.5 * bias_ref[pl.ds(layer, 1), pl.ds(C, C)])
            twice_gated = (filtered + filtered * gate).astype(BF16)
            all_gated[:, pl.ds(layer * C, C)] = twice_gated
            added = jnp.dot(twice_gated, res_proj[layer], preferred_element_type=F32)
            at_cur = pl.ds(PAD, LENGTH)
            if layer < LAYERS - 1:
                cur[at_cur, :] = cur[at_cur, :] + added
            else:
                result[0] = ((cur[at_cur, :] - start[...].astype(F32)) + added).astype(BF16)

    def skip_sums():
        sums = jnp.dot(all_gated[...], skip_proj[...], preferred_element_type=F32)
        result[1] = sums.astype(BF16)

    wide = (GROUP, 32, C)

    def leave_along_z(unit, part, stage):
        rows = reordered(turn512[...], result[part])
        leave[unit] = rows.astype(BF16).reshape(wide)
        exchange(leave.at[unit], passing.at[unit], True, stage)

    own = []

    def last_stage(unit, out, chunk, along_z, arrival, stage):
        wait_for(passing.at[unit], arrival)
        rows = reordered(join512[...], passing[unit].reshape(LENGTH, C))
        last[unit] = rows.astype(BF16).reshape(GROUP, HALVES, 16, C)
        mine = j if along_z else g
        owner = j if along_z else g
        at = pl.ds(pl.multiple_of(chunk * 256 + owner * 16, 16), 16)
        for peer in z_peers if along_z else xy_peers:
            send(last.at[unit, peer], out.at[:, at, :], peer, along_z, stage)
        copy = pltpu.make_async_copy(last.at[unit, mine], out.at[:, at, :], own_sem.at[unit])
        copy.start()
        own.append(copy)
        started[stage] = last.at[unit]

    wait_for(halves.at[0], 2)
    wait_for(halves.at[1], 4)
    rows = reordered(enter512[...], halves[...].reshape(LENGTH, C))
    cur[pl.ds(PAD, LENGTH), :] = rows
    start[...] = rows.astype(BF16)
    layers()
    leave_along_z(0, 0, 6)
    skip_sums()
    leave_along_z(1, 1, 7)

    wait_for(late, 5)
    rows = reordered(turn512[...], late[...].reshape(LENGTH, C))
    cur[pl.ds(PAD, LENGTH), :] = rows
    start[...] = rows.astype(BF16)
    layers()
    leave[2] = result[0].reshape(wide)
    exchange(leave.at[2], passing.at[2], False, 8)
    skip_sums()
    leave[3] = result[1].reshape(wide)
    exchange(leave.at[3], passing.at[3], False, 9)

    last_stage(2, delta_out, 1, True, 8, 12)
    last_stage(3, skip_out, 1, True, 9, 13)
    last_stage(0, delta_out, 0, False, 6, 10)
    last_stage(1, skip_out, 0, False, 7, 11)

    for unit, stage in ((0, 10), (1, 11), (2, 12), (3, 13)):
        wait_for(last.at[unit], stage)
    for copy in own:
        copy.wait()
    for stage, source in started.items():
        finish(source, send_sem.at[stage])


def finish_kernel(signal_ref, delta_ref, skip_in_ref, features_ref, skip_ref):
    first, second = pl.ds(0, 256), pl.ds(256, 256)
    features_ref[first, :] = signal_ref[first, :] + delta_ref[first, :].astype(F32)
    skip_ref[first, :] = skip_in_ref[first, :].astype(F32)
    swap = one_hot(256, lambda o: (o & 15) * 16 + (o >> 4))
    features_ref[second, :] = signal_ref[second, :] + reordered(swap, delta_ref[second, :])
    skip_ref[second, :] = reordered(swap, skip_in_ref[second, :])


def body(signal, conv_weight, conv_bias, res_weight, skip_weight):
    any_space = pl.BlockSpec(memory_space=pl.ANY)

    def vmem(*shape, dtype=BF16):
        return pltpu.VMEM(shape, dtype)

    delta, skip_sum = pl.pallas_call(
        kernel,
        out_shape=[jax.ShapeDtypeStruct((HALVES, RESIDUES, C), BF16)] * 2,
        in_specs=[any_space, any_space, pl.BlockSpec(memory_space=pltpu.VMEM), any_space, any_space],
        out_specs=[any_space, any_space],
        scratch_shapes=[
            vmem(HALVES, RESIDUES, C, dtype=F32),
            vmem(LAYERS, 3 * C, 2 * C),
            vmem(LAYERS, C, C),
            vmem(LAYERS * C, C),
            vmem(256, 256),
            vmem(LENGTH, LENGTH),
            vmem(LENGTH, LENGTH),
            vmem(LENGTH, LENGTH),
            vmem(LENGTH, LENGTH),
            vmem(GROUP, 16, C),
            vmem(GROUP, 16, C),
            vmem(GROUP, HALVES, 16, C),
            vmem(GROUP, 16, C),
            vmem(GROUP, 16, C),
            vmem(GROUP, 16, C),
            vmem(GROUP, 16, C),
            vmem(2, GROUP, 16, C),
            vmem(GROUP, HALVES, 16, C),
            vmem(GROUP, 32, C),
            vmem(GROUP, 32, C),
            vmem(4, GROUP, 32, C),
            vmem(4, GROUP, 32, C),
            vmem(4, GROUP, HALVES, 16, C),
            vmem(LENGTH + 2 * PAD, C, dtype=F32),
            vmem(LENGTH, LAYERS * C),
            vmem(LENGTH, C),
            vmem(2, LENGTH, C),
            vmem(LENGTH, 3 * C),
            pltpu.SemaphoreType.DMA,
            pltpu.SemaphoreType.DMA((3,)),
            pltpu.SemaphoreType.DMA((14,)),
            pltpu.SemaphoreType.DMA((14,)),
            pltpu.SemaphoreType.DMA((4,)),
        ],
        compiler_params=pltpu.CompilerParams(
            collective_id=0, has_side_effects=True, vmem_limit_bytes=60 * 2**20
        ),
    )(
        signal.reshape(HALVES, RESIDUES, C),
        conv_weight,
        conv_bias,
        res_weight,
        skip_weight.reshape(LAYERS * C, C),
    )
    block = pl.BlockSpec((RESIDUES, C), lambda i: (i, 0))
    shape = signal.shape
    return pl.pallas_call(
        finish_kernel,
        grid=(HALVES,),
        out_shape=[jax.ShapeDtypeStruct(shape, F32)] * 2,
        in_specs=[block, block, block],
        out_specs=[block, block],
    )(signal, delta.reshape(shape), skip_sum.reshape(shape))


def solution(mesh):
    in_specs = (P("seq", None), P(), P(), P(), P())
    out_specs = (P("seq", None), P("seq", None))
    return jax.shard_map(body, mesh=mesh, in_specs=in_specs, out_specs=out_specs, check_vma=False)
```

```python
import jax
import jax.numpy as jnp
from jax import lax
from jax.experimental import pallas as pl
from jax.experimental.pallas import tpu as pltpu
from jax.sharding import PartitionSpec as P

LAYERS = 6
HALVES = 2
RESIDUES = 512
GROUP = 16
LENGTH = 512
C = 256
PAD = 32
MESH = pl.DeviceIdType.MESH
BF16 = jnp.bfloat16
F32 = jnp.float32

ALONG_Z = [(dz, dc) for dz in (1, 7, 2, 6, 3, 5, 4, 0) for dc in (0, 1) if (dz, dc) != (0, 0)]
ACROSS = [(dy, dx) for dy in (0, 1, 3, 2) for dx in (1, 3, 2, 0) if (dy, dx) != (0, 0)]


def one_hot(rows, source):
    out = lax.broadcasted_iota(jnp.int32, (rows, rows), 0)
    col = lax.broadcasted_iota(jnp.int32, (rows, rows), 1)
    return jnp.where(col == source(out), 1.0, 0.0).astype(BF16)


def reordered(matrix, rows):
    return jnp.dot(matrix, rows, preferred_element_type=F32)


def kernel(
    signal_hbm,
    conv_hbm,
    bias_ref,
    res_hbm,
    skip_hbm,
    delta_out,
    skip_out,
    signal,
    conv,
    res_proj,
    skip_proj,
    swap256,
    join512,
    turn512,
    enter512,
    sent_xy,
    sent_z,
    late_sent_xy,
    late_sent_z,
    first_xy,
    first_z,
    next_z,
    next_xy,
    halves,
    late_first_xy,
    late_first_z,
    late_next_z,
    late_next_xy,
    late_halves,
    leave,
    passing,
    last,
    cur,
    all_gated,
    start,
    result,
    x3,
    load_sem,
    weight_sem,
    send_sem,
    recv_sem,
    own_sem,
):
    me = lax.axis_index("seq")
    j, g = lax.rem(me, GROUP), me // GROUP
    z, core = j // 2, lax.rem(j, 2)
    y, x = g // 4, lax.rem(g, 4)
    z_peers = [lax.rem(z + dz, 8) * 2 + lax.rem(core + dc, 2) for dz, dc in ALONG_Z]
    xy_peers = [lax.rem(y + dy, 4) * 4 + lax.rem(x + dx, 4) for dy, dx in ACROSS]

    barrier = pltpu.get_barrier_semaphore()
    for peer in z_peers:
        pl.semaphore_signal(barrier, inc=1, device_id=(g * GROUP + peer,), device_id_type=MESH)
    for peer in xy_peers:
        pl.semaphore_signal(barrier, inc=1, device_id=(peer * GROUP + j,), device_id_type=MESH)

    load = pltpu.make_async_copy(signal_hbm, signal, load_sem)
    load.start()
    weights = [
        pltpu.make_async_copy(conv_hbm, conv, weight_sem.at[0]),
        pltpu.make_async_copy(res_hbm, res_proj, weight_sem.at[1]),
        pltpu.make_async_copy(skip_hbm, skip_proj, weight_sem.at[2]),
    ]
    for copy in weights:
        copy.start()
    swap256[...] = one_hot(256, lambda o: (o & 15) * 16 + (o >> 4))
    join512[...] = one_hot(LENGTH, lambda o: (o & 15) * 32 + (o >> 4))
    turn512[...] = one_hot(LENGTH, lambda o: ((o >> 1) & 15) * 32 + (o >> 5) * 2 + (o & 1))
    enter512[...] = one_hot(
        LENGTH,
        lambda o: jnp.where(
            (o & 1) == 0, ((o >> 1) & 15) * 16 + (o >> 5), 256 + (o >> 5) * 16 + ((o >> 1) & 15)
        ),
    )
    cur[pl.ds(0, PAD), :] = jnp.zeros((PAD, C), F32)
    cur[pl.ds(PAD + LENGTH, PAD), :] = jnp.zeros((PAD, C), F32)
    load.wait()
    slab = (GROUP, 16, C)
    for chunk, across, along in ((0, sent_xy, sent_z), (1, late_sent_xy, late_sent_z)):
        at = pl.ds(chunk * 256, 256)
        across[...] = signal[0, at, :].astype(BF16).reshape(slab)
        rows = reordered(swap256[...], signal[1, at, :].astype(BF16))
        along[...] = rows.astype(BF16).reshape(slab)
    for copy in weights:
        copy.wait()
    for layer in range(LAYERS):
        conv[layer, :, pl.ds(C, C)] = conv[layer, :, pl.ds(C, C)] * jnp.asarray(0.5, BF16)
        res_proj[layer] = res_proj[layer] * jnp.asarray(0.5, BF16)
        at = pl.ds(layer * C, C)
        skip_proj[at, :] = skip_proj[at, :] * jnp.asarray(0.5, BF16)
    pl.semaphore_wait(barrier, 2 * (GROUP - 1))

    started = {}

    def send(src, dst, peer, along_z, stage):
        device = g * GROUP + peer if along_z else peer * GROUP + j
        pltpu.make_async_remote_copy(
            src_ref=src,
            dst_ref=dst,
            send_sem=send_sem.at[stage],
            recv_sem=recv_sem.at[stage],
            device_id=(device,),
            device_id_type=MESH,
        ).start()

    def exchange(source, target, along_z, stage):
        mine = j if along_z else g
        for peer in z_peers if along_z else xy_peers:
            send(source.at[peer], target.at[mine], peer, along_z, stage)
        target[mine] = source[mine]
        started[stage] = source

    def finish(source, sem):
        part = source.at[pl.ds(0, GROUP - 1)]
        pltpu.make_async_copy(part, part, sem).wait()

    def wait_for(target, stage):
        finish(target, recv_sem.at[stage])

    def leaves(source, stage):
        finish(source, send_sem.at[stage])
        del started[stage]

    def turned(arrived):
        rows = reordered(swap256[...], arrived[...].reshape(256, C))
        return rows.astype(BF16).reshape(slab)

    exchange(sent_xy, first_xy, False, 0)
    exchange(sent_z, first_z, True, 1)
    exchange(late_sent_xy, late_first_xy, False, 3)
    leaves(sent_z, 1)
    exchange(late_sent_z, late_first_z, True, 14)
    wait_for(first_xy, 0)
    next_z[...] = turned(first_xy)
    exchange(next_z, halves.at[0], True, 2)
    wait_for(first_z, 1)
    next_xy[...] = turned(first_z)
    exchange(next_xy, halves.at[1], False, 4)
    wait_for(late_first_xy, 3)
    late_next_z[...] = turned(late_first_xy)
    leaves(next_z, 2)
    exchange(late_next_z, late_halves.at[0], True, 5)
    wait_for(late_first_z, 14)
    late_next_xy[...] = turned(late_first_z)
    exchange(late_next_xy, late_halves.at[1], False, 15)

    def enter(arrived):
        rows = reordered(enter512[...], arrived[...].reshape(LENGTH, C))
        cur[pl.ds(PAD, LENGTH), :] = rows
        start[...] = rows.astype(BF16)

    def layers():
        for layer in range(LAYERS):
            d = 2**layer
            for tap in range(3):
                x3[:, pl.ds(tap * C, C)] = cur[pl.ds(PAD + (tap - 1) * d, LENGTH), :].astype(BF16)
            pre = jnp.dot(x3[...], conv[layer], preferred_element_type=F32)
            filtered = jnp.tanh(pre[:, :C] + bias_ref[pl.ds(layer, 1), pl.ds(0, C)])
            gate = jnp.tanh(pre[:, C:] + 0.5 * bias_ref[pl.ds(layer, 1), pl.ds(C, C)])
            twice_gated = (filtered + filtered * gate).astype(BF16)
            all_gated[:, pl.ds(layer * C, C)] = twice_gated
            added = jnp.dot(twice_gated, res_proj[layer], preferred_element_type=F32)
            at_cur = pl.ds(PAD, LENGTH)
            if layer < LAYERS - 1:
                cur[at_cur, :] = cur[at_cur, :] + added
            else:
                result[0] = ((cur[at_cur, :] - start[...].astype(F32)) + added).astype(BF16)

    def skip_sums():
        sums = jnp.dot(all_gated[...], skip_proj[...], preferred_element_type=F32)
        result[1] = sums.astype(BF16)

    wide = (GROUP, 32, C)

    def leave_along_z(unit, part, stage):
        rows = reordered(turn512[...], result[part])
        leave[unit] = rows.astype(BF16).reshape(wide)
        exchange(leave.at[unit], passing.at[unit], True, stage)

    own = []

    def last_stage(unit, out, chunk, along_z, arrival, stage):
        wait_for(passing.at[unit], arrival)
        rows = reordered(join512[...], passing[unit].reshape(LENGTH, C))
        last[unit] = rows.astype(BF16).reshape(GROUP, HALVES, 16, C)
        mine = j if along_z else g
        owner = j if along_z else g
        at = pl.ds(pl.multiple_of(chunk * 256 + owner * 16, 16), 16)
        for peer in z_peers if along_z else xy_peers:
            send(last.at[unit, peer], out.at[:, at, :], peer, along_z, stage)
        copy = pltpu.make_async_copy(last.at[unit, mine], out.at[:, at, :], own_sem.at[unit])
        copy.start()
        own.append(copy)
        started[stage] = last.at[unit]

    wait_for(halves.at[0], 2)
    wait_for(halves.at[1], 4)
    enter(halves)
    layers()
    leave_along_z(0, 0, 6)
    skip_sums()
    leave_along_z(1, 1, 7)

    wait_for(late_halves.at[0], 5)
    wait_for(late_halves.at[1], 15)
    enter(late_halves)
    layers()
    leave[2] = result[0].reshape(wide)
    exchange(leave.at[2], passing.at[2], False, 8)
    skip_sums()
    leave[3] = result[1].reshape(wide)
    exchange(leave.at[3], passing.at[3], False, 9)

    last_stage(2, delta_out, 1, True, 8, 12)
    last_stage(3, skip_out, 1, True, 9, 13)
    last_stage(0, delta_out, 0, False, 6, 10)
    last_stage(1, skip_out, 0, False, 7, 11)

    for unit, stage in ((0, 10), (1, 11), (2, 12), (3, 13)):
        wait_for(last.at[unit], stage)
    for copy in own:
        copy.wait()
    for stage, source in started.items():
        finish(source, send_sem.at[stage])


def finish_kernel(signal_ref, delta_ref, skip_in_ref, features_ref, skip_ref):
    first, second = pl.ds(0, 256), pl.ds(256, 256)
    features_ref[first, :] = signal_ref[first, :] + delta_ref[first, :].astype(F32)
    skip_ref[first, :] = skip_in_ref[first, :].astype(F32)
    swap = one_hot(256, lambda o: (o & 15) * 16 + (o >> 4))
    features_ref[second, :] = signal_ref[second, :] + reordered(swap, delta_ref[second, :])
    skip_ref[second, :] = reordered(swap, skip_in_ref[second, :])


def body(signal, conv_weight, conv_bias, res_weight, skip_weight):
    any_space = pl.BlockSpec(memory_space=pl.ANY)

    def vmem(*shape, dtype=BF16):
        return pltpu.VMEM(shape, dtype)

    delta, skip_sum = pl.pallas_call(
        kernel,
        out_shape=[jax.ShapeDtypeStruct((HALVES, RESIDUES, C), BF16)] * 2,
        in_specs=[any_space, any_space, pl.BlockSpec(memory_space=pltpu.VMEM), any_space, any_space],
        out_specs=[any_space, any_space],
        scratch_shapes=[
            vmem(HALVES, RESIDUES, C, dtype=F32),
            vmem(LAYERS, 3 * C, 2 * C),
            vmem(LAYERS, C, C),
            vmem(LAYERS * C, C),
            vmem(256, 256),
            vmem(LENGTH, LENGTH),
            vmem(LENGTH, LENGTH),
            vmem(LENGTH, LENGTH),
            vmem(GROUP, 16, C),
            vmem(GROUP, 16, C),
            vmem(GROUP, 16, C),
            vmem(GROUP, 16, C),
            vmem(GROUP, 16, C),
            vmem(GROUP, 16, C),
            vmem(GROUP, 16, C),
            vmem(GROUP, 16, C),
            vmem(2, GROUP, 16, C),
            vmem(GROUP, 16, C),
            vmem(GROUP, 16, C),
            vmem(GROUP, 16, C),
            vmem(GROUP, 16, C),
            vmem(2, GROUP, 16, C),
            vmem(4, GROUP, 32, C),
            vmem(4, GROUP, 32, C),
            vmem(4, GROUP, HALVES, 16, C),
            vmem(LENGTH + 2 * PAD, C, dtype=F32),
            vmem(LENGTH, LAYERS * C),
            vmem(LENGTH, C),
            vmem(2, LENGTH, C),
            vmem(LENGTH, 3 * C),
            pltpu.SemaphoreType.DMA,
            pltpu.SemaphoreType.DMA((3,)),
            pltpu.SemaphoreType.DMA((16,)),
            pltpu.SemaphoreType.DMA((16,)),
            pltpu.SemaphoreType.DMA((4,)),
        ],
        compiler_params=pltpu.CompilerParams(
            collective_id=0, has_side_effects=True, vmem_limit_bytes=60 * 2**20
        ),
    )(
        signal.reshape(HALVES, RESIDUES, C),
        conv_weight,
        conv_bias,
        res_weight,
        skip_weight.reshape(LAYERS * C, C),
    )
    block = pl.BlockSpec((RESIDUES, C), lambda i: (i, 0))
    shape = signal.shape
    return pl.pallas_call(
        finish_kernel,
        grid=(HALVES,),
        out_shape=[jax.ShapeDtypeStruct(shape, F32)] * 2,
        in_specs=[block, block, block],
        out_specs=[block, block],
    )(signal, delta.reshape(shape), skip_sum.reshape(shape))


def solution(mesh):
    in_specs = (P("seq", None), P(), P(), P(), P())
    out_specs = (P("seq", None), P("seq", None))
    return jax.shard_map(body, mesh=mesh, in_specs=in_specs, out_specs=out_specs, check_vma=False)
```

```python
import jax
import jax.numpy as jnp
from jax import lax
from jax.experimental import pallas as pl
from jax.experimental.pallas import tpu as pltpu
from jax.sharding import PartitionSpec as P

LAYERS = 6
HALVES = 2
RESIDUES = 512
GROUP = 16
LENGTH = 512
C = 256
PAD = 32
MESH = pl.DeviceIdType.MESH
BF16 = jnp.bfloat16
F32 = jnp.float32

ALONG_Z = [(dz, dc) for dz in (1, 7, 2, 6, 3, 5, 4, 0) for dc in (0, 1) if (dz, dc) != (0, 0)]
ACROSS = [(dy, dx) for dy in (0, 1, 3, 2) for dx in (1, 3, 2, 0) if (dy, dx) != (0, 0)]


def one_hot(rows, source):
    out = lax.broadcasted_iota(jnp.int32, (rows, rows), 0)
    col = lax.broadcasted_iota(jnp.int32, (rows, rows), 1)
    return jnp.where(col == source(out), 1.0, 0.0).astype(BF16)


def reordered(matrix, rows):
    return jnp.dot(matrix, rows, preferred_element_type=F32)


def kernel(
    signal_hbm,
    conv_hbm,
    bias_hbm,
    res_hbm,
    skip_hbm,
    delta_out,
    skip_out,
    signal,
    conv,
    bias_ref,
    res_proj,
    skip_proj,
    swap256,
    split512,
    join512,
    turn512,
    enter512,
    sent_xy,
    sent_z,
    sent_late,
    first_xy,
    first_z,
    next_z,
    next_xy,
    halves,
    late_first,
    late_next,
    late,
    leave,
    passing,
    last,
    cur,
    all_gated,
    start,
    result,
    x3,
    load_sem,
    weight_sem,
    send_sem,
    recv_sem,
    own_sem,
):
    me = lax.axis_index("seq")
    j, g = lax.rem(me, GROUP), me // GROUP
    z, core = j // 2, lax.rem(j, 2)
    y, x = g // 4, lax.rem(g, 4)
    z_peers = [lax.rem(z + dz, 8) * 2 + lax.rem(core + dc, 2) for dz, dc in ALONG_Z]
    xy_peers = [lax.rem(y + dy, 4) * 4 + lax.rem(x + dx, 4) for dy, dx in ACROSS]

    barrier = pltpu.get_barrier_semaphore()
    for peer in z_peers:
        pl.semaphore_signal(barrier, inc=1, device_id=(g * GROUP + peer,), device_id_type=MESH)
    for peer in xy_peers:
        pl.semaphore_signal(barrier, inc=1, device_id=(peer * GROUP + j,), device_id_type=MESH)

    load = pltpu.make_async_copy(signal_hbm, signal, load_sem)
    load.start()
    weights = [
        pltpu.make_async_copy(conv_hbm, conv, weight_sem.at[0]),
        pltpu.make_async_copy(res_hbm, res_proj, weight_sem.at[1]),
        pltpu.make_async_copy(skip_hbm, skip_proj, weight_sem.at[2]),
        pltpu.make_async_copy(bias_hbm, bias_ref, weight_sem.at[3]),
    ]
    for copy in weights:
        copy.start()
    swap256[...] = one_hot(256, lambda o: (o & 15) * 16 + (o >> 4))
    split512[...] = one_hot(LENGTH, lambda o: (o & 31) * 16 + (o >> 5))
    join512[...] = one_hot(LENGTH, lambda o: (o & 15) * 32 + (o >> 4))
    turn512[...] = one_hot(LENGTH, lambda o: ((o >> 1) & 15) * 32 + (o >> 5) * 2 + (o & 1))
    enter512[...] = one_hot(
        LENGTH,
        lambda o: jnp.where(
            (o & 1) == 0, ((o >> 1) & 15) * 16 + (o >> 5), 256 + (o >> 5) * 16 + ((o >> 1) & 15)
        ),
    )
    cur[pl.ds(0, PAD), :] = jnp.zeros((PAD, C), F32)
    cur[pl.ds(PAD + LENGTH, PAD), :] = jnp.zeros((PAD, C), F32)
    load.wait()
    slab = (GROUP, 16, C)
    sent_xy[...] = signal[0, pl.ds(0, 256), :].astype(BF16).reshape(slab)
    sent_z[...] = reordered(swap256[...], signal[1, pl.ds(0, 256), :].astype(BF16)).astype(BF16).reshape(slab)
    for half in range(HALVES):
        sent_late[:, half] = signal[half, pl.ds(256, 256), :].astype(BF16).reshape(slab)
    for copy in weights:
        copy.wait()
    for layer in range(LAYERS):
        conv[layer, :, pl.ds(C, C)] = conv[layer, :, pl.ds(C, C)] * jnp.asarray(0.5, BF16)
        res_proj[layer] = res_proj[layer] * jnp.asarray(0.5, BF16)
        at = pl.ds(layer * C, C)
        skip_proj[at, :] = skip_proj[at, :] * jnp.asarray(0.5, BF16)
    pl.semaphore_wait(barrier, 2 * (GROUP - 1))

    started = {}

    def send(src, dst, peer, along_z, stage):
        device = g * GROUP + peer if along_z else peer * GROUP + j
        pltpu.make_async_remote_copy(
            src_ref=src,
            dst_ref=dst,
            send_sem=send_sem.at[stage],
            recv_sem=recv_sem.at[stage],
            device_id=(device,),
            device_id_type=MESH,
        ).start()

    def exchange(source, target, along_z, stage):
        mine = j if along_z else g
        for peer in z_peers if along_z else xy_peers:
            send(source.at[peer], target.at[mine], peer, along_z, stage)
        target[mine] = source[mine]
        started[stage] = source

    def finish(source, sem):
        part = source.at[pl.ds(0, GROUP - 1)]
        pltpu.make_async_copy(part, part, sem).wait()

    def wait_for(target, stage):
        finish(target, recv_sem.at[stage])

    exchange(sent_xy, first_xy, False, 0)
    exchange(sent_z, first_z, True, 1)
    exchange(sent_late, late_first, False, 3)
    wait_for(first_xy, 0)
    next_z[...] = reordered(swap256[...], first_xy[...].reshape(256, C)).astype(BF16).reshape(slab)
    exchange(next_z, halves.at[0], True, 2)
    wait_for(first_z, 1)
    next_xy[...] = reordered(swap256[...], first_z[...].reshape(256, C)).astype(BF16).reshape(slab)
    exchange(next_xy, halves.at[1], False, 4)
    wait_for(late_first, 3)
    rows = reordered(split512[...], late_first[...].reshape(LENGTH, C))
    late_next[...] = rows.astype(BF16).reshape(GROUP, 32, C)
    exchange(late_next, late, True, 5)

    def layers():
        for layer in range(LAYERS):
            d = 2**layer
            for tap in range(3):
                x3[:, pl.ds(tap * C, C)] = cur[pl.ds(PAD + (tap - 1) * d, LENGTH), :].astype(BF16)
            pre = jnp.dot(x3[...], conv[layer], preferred_element_type=F32)
            filtered = jnp.tanh(pre[:, :C] + bias_ref[pl.ds(layer, 1), pl.ds(0, C)])
            gate = jnp.tanh(pre[:, C:] + 0.5 * bias_ref[pl.ds(layer, 1), pl.ds(C, C)])
            twice_gated = (filtered + filtered * gate).astype(BF16)
            all_gated[:, pl.ds(layer * C, C)] = twice_gated
            added = jnp.dot(twice_gated, res_proj[layer], preferred_element_type=F32)
            at_cur = pl.ds(PAD, LENGTH)
            if layer < LAYERS - 1:
                cur[at_cur, :] = cur[at_cur, :] + added
            else:
                result[0] = ((cur[at_cur, :] - start[...].astype(F32)) + added).astype(BF16)

    def skip_sums():
        sums = jnp.dot(all_gated[...], skip_proj[...], preferred_element_type=F32)
        result[1] = sums.astype(BF16)

    wide = (GROUP, 32, C)

    def leave_along_z(unit, part, stage):
        rows = reordered(turn512[...], result[part])
        leave[unit] = rows.astype(BF16).reshape(wide)
        exchange(leave.at[unit], passing.at[unit], True, stage)

    own = []

    def last_stage(unit, out, chunk, along_z, arrival, stage):
        wait_for(passing.at[unit], arrival)
        rows = reordered(join512[...], passing[unit].reshape(LENGTH, C))
        last[unit] = rows.astype(BF16).reshape(GROUP, HALVES, 16, C)
        mine = j if along_z else g
        owner = j if along_z else g
        at = pl.ds(pl.multiple_of(chunk * 256 + owner * 16, 16), 16)
        for peer in z_peers if along_z else xy_peers:
            send(last.at[unit, peer], out.at[:, at, :], peer, along_z, stage)
        copy = pltpu.make_async_copy(last.at[unit, mine], out.at[:, at, :], own_sem.at[unit])
        copy.start()
        own.append(copy)
        started[stage] = last.at[unit]

    wait_for(halves.at[0], 2)
    wait_for(halves.at[1], 4)
    rows = reordered(enter512[...], halves[...].reshape(LENGTH, C))
    cur[pl.ds(PAD, LENGTH), :] = rows
    start[...] = rows.astype(BF16)
    layers()
    leave_along_z(0, 0, 6)
    skip_sums()
    leave_along_z(1, 1, 7)

    wait_for(late, 5)
    rows = reordered(turn512[...], late[...].reshape(LENGTH, C))
    cur[pl.ds(PAD, LENGTH), :] = rows
    start[...] = rows.astype(BF16)
    layers()
    leave[2] = result[0].reshape(wide)
    exchange(leave.at[2], passing.at[2], False, 8)
    skip_sums()
    leave[3] = result[1].reshape(wide)
    exchange(leave.at[3], passing.at[3], False, 9)

    last_stage(2, delta_out, 1, True, 8, 12)
    last_stage(3, skip_out, 1, True, 9, 13)
    last_stage(0, delta_out, 0, False, 6, 10)
    last_stage(1, skip_out, 0, False, 7, 11)

    for unit, stage in ((0, 10), (1, 11), (2, 12), (3, 13)):
        wait_for(last.at[unit], stage)
    for copy in own:
        copy.wait()
    for stage, source in started.items():
        finish(source, send_sem.at[stage])


def finish_kernel(signal_ref, delta_ref, skip_in_ref, features_ref, skip_ref):
    first, second = pl.ds(0, 256), pl.ds(256, 256)
    features_ref[first, :] = signal_ref[first, :] + delta_ref[first, :].astype(F32)
    skip_ref[first, :] = skip_in_ref[first, :].astype(F32)
    swap = one_hot(256, lambda o: (o & 15) * 16 + (o >> 4))
    features_ref[second, :] = signal_ref[second, :] + reordered(swap, delta_ref[second, :])
    skip_ref[second, :] = reordered(swap, skip_in_ref[second, :])


def body(signal, conv_weight, conv_bias, res_weight, skip_weight):
    any_space = pl.BlockSpec(memory_space=pl.ANY)

    def vmem(*shape, dtype=BF16):
        return pltpu.VMEM(shape, dtype)

    delta, skip_sum = pl.pallas_call(
        kernel,
        out_shape=[jax.ShapeDtypeStruct((HALVES, RESIDUES, C), BF16)] * 2,
        in_specs=[any_space] * 5,
        out_specs=[any_space, any_space],
        scratch_shapes=[
            vmem(HALVES, RESIDUES, C, dtype=F32),
            vmem(LAYERS, 3 * C, 2 * C),
            vmem(LAYERS, 2 * C, dtype=F32),
            vmem(LAYERS, C, C),
            vmem(LAYERS * C, C),
            vmem(256, 256),
            vmem(LENGTH, LENGTH),
            vmem(LENGTH, LENGTH),
            vmem(LENGTH, LENGTH),
            vmem(LENGTH, LENGTH),
            vmem(GROUP, 16, C),
            vmem(GROUP, 16, C),
            vmem(GROUP, HALVES, 16, C),
            vmem(GROUP, 16, C),
            vmem(GROUP, 16, C),
            vmem(GROUP, 16, C),
            vmem(GROUP, 16, C),
            vmem(2, GROUP, 16, C),
            vmem(GROUP, HALVES, 16, C),
            vmem(GROUP, 32, C),
            vmem(GROUP, 32, C),
            vmem(4, GROUP, 32, C),
            vmem(4, GROUP, 32, C),
            vmem(4, GROUP, HALVES, 16, C),
            vmem(LENGTH + 2 * PAD, C, dtype=F32),
            vmem(LENGTH, LAYERS * C),
            vmem(LENGTH, C),
            vmem(2, LENGTH, C),
            vmem(LENGTH, 3 * C),
            pltpu.SemaphoreType.DMA,
            pltpu.SemaphoreType.DMA((4,)),
            pltpu.SemaphoreType.DMA((14,)),
            pltpu.SemaphoreType.DMA((14,)),
            pltpu.SemaphoreType.DMA((4,)),
        ],
        compiler_params=pltpu.CompilerParams(
            collective_id=0, has_side_effects=True, vmem_limit_bytes=60 * 2**20
        ),
    )(
        signal.reshape(HALVES, RESIDUES, C),
        conv_weight,
        conv_bias,
        res_weight,
        skip_weight.reshape(LAYERS * C, C),
    )
    block = pl.BlockSpec((RESIDUES, C), lambda i: (i, 0))
    shape = signal.shape
    return pl.pallas_call(
        finish_kernel,
        grid=(HALVES,),
        out_shape=[jax.ShapeDtypeStruct(shape, F32)] * 2,
        in_specs=[block, block, block],
        out_specs=[block, block],
    )(signal, delta.reshape(shape), skip_sum.reshape(shape))


def solution(mesh):
    in_specs = (P("seq", None), P(), P(), P(), P())
    out_specs = (P("seq", None), P("seq", None))
    return jax.shard_map(body, mesh=mesh, in_specs=in_specs, out_specs=out_specs, check_vma=False)
```

```python
import jax
import jax.numpy as jnp
from jax import lax
from jax.experimental import pallas as pl
from jax.experimental.pallas import tpu as pltpu
from jax.sharding import PartitionSpec as P

LAYERS = 6
HALVES = 2
RESIDUES = 512
GROUP = 16
LENGTH = 512
C = 256
PAD = 32
MESH = pl.DeviceIdType.MESH
BF16 = jnp.bfloat16
F32 = jnp.float32

ALONG_Z = [(dz, dc) for dz in (1, 7, 2, 6, 3, 5, 4, 0) for dc in (0, 1) if (dz, dc) != (0, 0)]
ACROSS = [(dy, dx) for dy in (0, 1, 3, 2) for dx in (1, 3, 2, 0) if (dy, dx) != (0, 0)]


def one_hot(rows, source):
    out = lax.broadcasted_iota(jnp.int32, (rows, rows), 0)
    col = lax.broadcasted_iota(jnp.int32, (rows, rows), 1)
    return jnp.where(col == source(out), 1.0, 0.0).astype(BF16)


def reordered(matrix, rows):
    return jnp.dot(matrix, rows, preferred_element_type=F32)


def kernel(
    signal_hbm,
    conv_hbm,
    bias_hbm,
    res_hbm,
    skip_hbm,
    delta_out,
    skip_out,
    signal,
    conv,
    bias_ref,
    res_proj,
    skip_proj,
    swap256,
    split512,
    join512,
    turn512,
    enter512,
    sent_xy,
    sent_z,
    sent_late,
    first_xy,
    first_z,
    next_z,
    next_xy,
    halves,
    late_first,
    late_next,
    late,
    leave,
    passing,
    last,
    cur,
    all_gated,
    start,
    result,
    x3,
    load_sem,
    weight_sem,
    send_sem,
    recv_sem,
    own_sem,
):
    me = lax.axis_index("seq")
    j, g = lax.rem(me, GROUP), me // GROUP
    z, core = j // 2, lax.rem(j, 2)
    y, x = g // 4, lax.rem(g, 4)
    z_peers = [lax.rem(z + dz, 8) * 2 + lax.rem(core + dc, 2) for dz, dc in ALONG_Z]
    xy_peers = [lax.rem(y + dy, 4) * 4 + lax.rem(x + dx, 4) for dy, dx in ACROSS]

    barrier = pltpu.get_barrier_semaphore()
    for peer in z_peers:
        pl.semaphore_signal(barrier, inc=1, device_id=(g * GROUP + peer,), device_id_type=MESH)
    for peer in xy_peers:
        pl.semaphore_signal(barrier, inc=1, device_id=(peer * GROUP + j,), device_id_type=MESH)

    load = pltpu.make_async_copy(signal_hbm, signal, load_sem)
    load.start()
    weights = [
        pltpu.make_async_copy(conv_hbm, conv, weight_sem.at[0]),
        pltpu.make_async_copy(res_hbm, res_proj, weight_sem.at[1]),
        pltpu.make_async_copy(skip_hbm, skip_proj, weight_sem.at[2]),
        pltpu.make_async_copy(bias_hbm, bias_ref, weight_sem.at[3]),
    ]
    for copy in weights:
        copy.start()
    swap256[...] = one_hot(256, lambda o: (o & 15) * 16 + (o >> 4))
    cur[pl.ds(0, PAD), :] = jnp.zeros((PAD, C), F32)
    cur[pl.ds(PAD + LENGTH, PAD), :] = jnp.zeros((PAD, C), F32)
    load.wait()
    slab = (GROUP, 16, C)
    sent_xy[...] = signal[0, pl.ds(0, 256), :].astype(BF16).reshape(slab)
    sent_z[...] = reordered(swap256[...], signal[1, pl.ds(0, 256), :].astype(BF16)).astype(BF16).reshape(slab)
    for half in range(HALVES):
        sent_late[:, half] = signal[half, pl.ds(256, 256), :].astype(BF16).reshape(slab)
    pl.semaphore_wait(barrier, 2 * (GROUP - 1))

    started = {}

    def send(src, dst, peer, along_z, stage):
        device = g * GROUP + peer if along_z else peer * GROUP + j
        pltpu.make_async_remote_copy(
            src_ref=src,
            dst_ref=dst,
            send_sem=send_sem.at[stage],
            recv_sem=recv_sem.at[stage],
            device_id=(device,),
            device_id_type=MESH,
        ).start()

    def exchange(source, target, along_z, stage):
        mine = j if along_z else g
        for peer in z_peers if along_z else xy_peers:
            send(source.at[peer], target.at[mine], peer, along_z, stage)
        target[mine] = source[mine]
        started[stage] = source

    def finish(source, sem):
        part = source.at[pl.ds(0, GROUP - 1)]
        pltpu.make_async_copy(part, part, sem).wait()

    def wait_for(target, stage):
        finish(target, recv_sem.at[stage])

    exchange(sent_xy, first_xy, False, 0)
    exchange(sent_z, first_z, True, 1)
    exchange(sent_late, late_first, False, 3)
    split512[...] = one_hot(LENGTH, lambda o: (o & 31) * 16 + (o >> 5))
    join512[...] = one_hot(LENGTH, lambda o: (o & 15) * 32 + (o >> 4))
    turn512[...] = one_hot(LENGTH, lambda o: ((o >> 1) & 15) * 32 + (o >> 5) * 2 + (o & 1))
    enter512[...] = one_hot(
        LENGTH,
        lambda o: jnp.where(
            (o & 1) == 0, ((o >> 1) & 15) * 16 + (o >> 5), 256 + (o >> 5) * 16 + ((o >> 1) & 15)
        ),
    )
    for copy in weights:
        copy.wait()
    for layer in range(LAYERS):
        conv[layer, :, pl.ds(C, C)] = conv[layer, :, pl.ds(C, C)] * jnp.asarray(0.5, BF16)
        res_proj[layer] = res_proj[layer] * jnp.asarray(0.5, BF16)
        at = pl.ds(layer * C, C)
        skip_proj[at, :] = skip_proj[at, :] * jnp.asarray(0.5, BF16)
    wait_for(first_xy, 0)
    next_z[...] = reordered(swap256[...], first_xy[...].reshape(256, C)).astype(BF16).reshape(slab)
    exchange(next_z, halves.at[0], True, 2)
    wait_for(first_z, 1)
    next_xy[...] = reordered(swap256[...], first_z[...].reshape(256, C)).astype(BF16).reshape(slab)
    exchange(next_xy, halves.at[1], False, 4)
    wait_for(late_first, 3)
    rows = reordered(split512[...], late_first[...].reshape(LENGTH, C))
    late_next[...] = rows.astype(BF16).reshape(GROUP, 32, C)
    exchange(late_next, late, True, 5)

    def layers():
        for layer in range(LAYERS):
            d = 2**layer
            for tap in range(3):
                x3[:, pl.ds(tap * C, C)] = cur[pl.ds(PAD + (tap - 1) * d, LENGTH), :].astype(BF16)
            pre = jnp.dot(x3[...], conv[layer], preferred_element_type=F32)
            filtered = jnp.tanh(pre[:, :C] + bias_ref[pl.ds(layer, 1), pl.ds(0, C)])
            gate = jnp.tanh(pre[:, C:] + 0.5 * bias_ref[pl.ds(layer, 1), pl.ds(C, C)])
            twice_gated = (filtered + filtered * gate).astype(BF16)
            all_gated[:, pl.ds(layer * C, C)] = twice_gated
            added = jnp.dot(twice_gated, res_proj[layer], preferred_element_type=F32)
            at_cur = pl.ds(PAD, LENGTH)
            if layer < LAYERS - 1:
                cur[at_cur, :] = cur[at_cur, :] + added
            else:
                result[0] = ((cur[at_cur, :] - start[...].astype(F32)) + added).astype(BF16)

    def skip_sums():
        sums = jnp.dot(all_gated[...], skip_proj[...], preferred_element_type=F32)
        result[1] = sums.astype(BF16)

    wide = (GROUP, 32, C)

    def leave_along_z(unit, part, stage):
        rows = reordered(turn512[...], result[part])
        leave[unit] = rows.astype(BF16).reshape(wide)
        exchange(leave.at[unit], passing.at[unit], True, stage)

    own = []

    def last_stage(unit, out, chunk, along_z, arrival, stage):
        wait_for(passing.at[unit], arrival)
        rows = reordered(join512[...], passing[unit].reshape(LENGTH, C))
        last[unit] = rows.astype(BF16).reshape(GROUP, HALVES, 16, C)
        mine = j if along_z else g
        owner = j if along_z else g
        at = pl.ds(pl.multiple_of(chunk * 256 + owner * 16, 16), 16)
        for peer in z_peers if along_z else xy_peers:
            send(last.at[unit, peer], out.at[:, at, :], peer, along_z, stage)
        copy = pltpu.make_async_copy(last.at[unit, mine], out.at[:, at, :], own_sem.at[unit])
        copy.start()
        own.append(copy)
        started[stage] = last.at[unit]

    wait_for(halves.at[0], 2)
    wait_for(halves.at[1], 4)
    rows = reordered(enter512[...], halves[...].reshape(LENGTH, C))
    cur[pl.ds(PAD, LENGTH), :] = rows
    start[...] = rows.astype(BF16)
    layers()
    leave_along_z(0, 0, 6)
    skip_sums()
    leave_along_z(1, 1, 7)

    wait_for(late, 5)
    rows = reordered(turn512[...], late[...].reshape(LENGTH, C))
    cur[pl.ds(PAD, LENGTH), :] = rows
    start[...] = rows.astype(BF16)
    layers()
    leave[2] = result[0].reshape(wide)
    exchange(leave.at[2], passing.at[2], False, 8)
    skip_sums()
    leave[3] = result[1].reshape(wide)
    exchange(leave.at[3], passing.at[3], False, 9)

    last_stage(2, delta_out, 1, True, 8, 12)
    last_stage(3, skip_out, 1, True, 9, 13)
    last_stage(0, delta_out, 0, False, 6, 10)
    last_stage(1, skip_out, 0, False, 7, 11)

    for unit, stage in ((0, 10), (1, 11), (2, 12), (3, 13)):
        wait_for(last.at[unit], stage)
    for copy in own:
        copy.wait()
    for stage, source in started.items():
        finish(source, send_sem.at[stage])


def finish_kernel(signal_ref, delta_ref, skip_in_ref, features_ref, skip_ref):
    first, second = pl.ds(0, 256), pl.ds(256, 256)
    features_ref[first, :] = signal_ref[first, :] + delta_ref[first, :].astype(F32)
    skip_ref[first, :] = skip_in_ref[first, :].astype(F32)
    swap = one_hot(256, lambda o: (o & 15) * 16 + (o >> 4))
    features_ref[second, :] = signal_ref[second, :] + reordered(swap, delta_ref[second, :])
    skip_ref[second, :] = reordered(swap, skip_in_ref[second, :])


def body(signal, conv_weight, conv_bias, res_weight, skip_weight):
    any_space = pl.BlockSpec(memory_space=pl.ANY)

    def vmem(*shape, dtype=BF16):
        return pltpu.VMEM(shape, dtype)

    delta, skip_sum = pl.pallas_call(
        kernel,
        out_shape=[jax.ShapeDtypeStruct((HALVES, RESIDUES, C), BF16)] * 2,
        in_specs=[any_space] * 5,
        out_specs=[any_space, any_space],
        scratch_shapes=[
            vmem(HALVES, RESIDUES, C, dtype=F32),
            vmem(LAYERS, 3 * C, 2 * C),
            vmem(LAYERS, 2 * C, dtype=F32),
            vmem(LAYERS, C, C),
            vmem(LAYERS * C, C),
            vmem(256, 256),
            vmem(LENGTH, LENGTH),
            vmem(LENGTH, LENGTH),
            vmem(LENGTH, LENGTH),
            vmem(LENGTH, LENGTH),
            vmem(GROUP, 16, C),
            vmem(GROUP, 16, C),
            vmem(GROUP, HALVES, 16, C),
            vmem(GROUP, 16, C),
            vmem(GROUP, 16, C),
            vmem(GROUP, 16, C),
            vmem(GROUP, 16, C),
            vmem(2, GROUP, 16, C),
            vmem(GROUP, HALVES, 16, C),
            vmem(GROUP, 32, C),
            vmem(GROUP, 32, C),
            vmem(4, GROUP, 32, C),
            vmem(4, GROUP, 32, C),
            vmem(4, GROUP, HALVES, 16, C),
            vmem(LENGTH + 2 * PAD, C, dtype=F32),
            vmem(LENGTH, LAYERS * C),
            vmem(LENGTH, C),
            vmem(2, LENGTH, C),
            vmem(LENGTH, 3 * C),
            pltpu.SemaphoreType.DMA,
            pltpu.SemaphoreType.DMA((4,)),
            pltpu.SemaphoreType.DMA((14,)),
            pltpu.SemaphoreType.DMA((14,)),
            pltpu.SemaphoreType.DMA((4,)),
        ],
        compiler_params=pltpu.CompilerParams(
            collective_id=0, has_side_effects=True, vmem_limit_bytes=60 * 2**20
        ),
    )(
        signal.reshape(HALVES, RESIDUES, C),
        conv_weight,
        conv_bias,
        res_weight,
        skip_weight.reshape(LAYERS * C, C),
    )
    block = pl.BlockSpec((RESIDUES, C), lambda i: (i, 0))
    shape = signal.shape
    return pl.pallas_call(
        finish_kernel,
        grid=(HALVES,),
        out_shape=[jax.ShapeDtypeStruct(shape, F32)] * 2,
        in_specs=[block, block, block],
        out_specs=[block, block],
    )(signal, delta.reshape(shape), skip_sum.reshape(shape))


def solution(mesh):
    in_specs = (P("seq", None), P(), P(), P(), P())
    out_specs = (P("seq", None), P("seq", None))
    return jax.shard_map(body, mesh=mesh, in_specs=in_specs, out_specs=out_specs, check_vma=False)
```
